256 devices in a mesh: shot: 8 (over z_lo, core), probe: 32 (over x, z_hi, y).
Axes of the slice: x: 4, y: 4, z: 8 (z_hi: 2, z_lo: 4; z = z_hi * 4 + z_lo), core: 2. Of those that a mesh axis runs over, the one named last changes fastest.
Arguments:
- probes: float32 [64, 512, 512], P('probe'), may hold values from -6 to 6
- coarse_sample: float32 [64, 512, 512], P('probe', 'shot'), may hold values from -6 to 6
- coefficient: float32 [512, 512], replicated, may hold values from 0.05 to 0.45
- receiver: float32 [512, 512], replicated, may hold values from 0.05 to 0.5
- checkpoints: float32 [16, 2, 512, 512], P('shot', None, 'probe'), may hold values from -6 to 6
- encodings: int32 [16, 256], P('shot'), may hold values from -1 to 1, as said below
- wavelet: float32 [3, 256], replicated, may hold values from -6 to 6
- bounds: int32 [65], replicated, may hold values from 0 to 512, as said below
Outputs:
- samples: float32 [64, 512, 512], P('probe', 'shot')
The draws below stay inside these ranges and needn't reach their ends.
Inputs may be any that keep to these rules, and one draw needn't show every extreme that they name: `encodings`: every entry is -1 or 1. bounds[0] = 0 and bounds[64] = 512; the entries rise strictly; blocks 2 i and 2 i + 1 together hold exactly 16 rows.
All inputs are finite; a program needn't handle non-finite values.
Results may differ from the reference program's by a relative error of at most 0.000094.
Values sent between devices are 32-bit elements; how exact they have to be, the bound alone decides.
No kernel may reach another device: no remote copies, remote signals or barrier semaphores. Data moves between devices by JAX's collectives and lax.ppermute only.
A program may use at most 128 MiB of HBM per device.

```python
import math
import jax
import jax.numpy as jnp
from jax import lax

NZ = 512
NSHOT = 256
NT = 4
BLK = 8
NX = 512
SUPER = 16
PROBES = 64
NB = 64


def draw_encodings(key, part):
    signs = jax.random.randint(key, (SUPER, NSHOT), 0, 2)
    return (signs * 2 - 1).astype(jnp.int32)


def draw_bounds(key, part):
    half = BLK // 2
    offset = jax.random.randint(key, (NB // 2,), 1 - half, half)
    sizes = jnp.stack([BLK + offset, BLK - offset], axis=1).reshape(-1)
    return jnp.concatenate([jnp.zeros((1,), jnp.int32), jnp.cumsum(sizes).astype(jnp.int32)])


def block_scale(rng, extent, pieces, smallest, high):
    def one(dim, parts):
        steps = jax.random.uniform(jax.random.fold_in(jax.random.fold_in(rng, 6), dim), (parts,), jnp.float32, smallest / len(pieces), high / len(pieces))
        return jnp.repeat(jnp.exp(steps), extent[dim] // parts).reshape((-1,) + (1,) * (len(extent) - dim - 1))

    factor_of = one(*pieces[0])
    for cut in pieces[1:]:
        factor_of = factor_of * one(*cut)
    return factor_of


def gaussian(key, dims, spread, limit, shards=(), held_as=jnp.bfloat16):
    result = spread * jax.random.normal(key, dims, jnp.float32)
    if shards:
        result = result * block_scale(key, dims, shards, -0.22, 0.18)
    return jnp.clip(result, -limit, limit).astype(held_as)


def setup_inputs(seed: int = 0) -> dict:
    streams_of = jax.random.split(jax.random.key(seed), 9)
    return {
        "probes": gaussian(streams_of[0], (PROBES, NX, NZ), 1.0, 6.0, ((0, 32),), jnp.float32),
        "coarse_sample": gaussian(streams_of[1], (PROBES, NX, NZ), 1.0, 6.0, ((0, 32), (1, 8)), jnp.float32),
        "coefficient": jnp.clip(jnp.exp(jax.random.uniform(streams_of[2], (NX, NZ), jnp.float32, math.log(0.05), math.log(0.45))), 0.05, 0.45),
        "receiver": jnp.clip(jnp.exp(jax.random.uniform(streams_of[3], (NX, NZ), jnp.float32, math.log(0.05), math.log(0.5))), 0.05, 0.5),
        "checkpoints": gaussian(streams_of[4], (SUPER, 2, NX, NZ), 1.0, 6.0, ((0, 8), (2, 32)), jnp.float32),
        "encodings": draw_encodings(jax.random.fold_in(streams_of[8], 71), 0),
        "wavelet": gaussian(streams_of[6], (NT - 1, NSHOT), 1.0, 6.0, (), jnp.float32),
        "bounds": draw_bounds(jax.random.fold_in(streams_of[8], 71), 0),
    }


def laplace(values):
    pad_width = [(0, 0)] * (values.ndim - 2) + [(1, 1), (1, 1)]
    padded = jnp.pad(values, pad_width)
    return padded[..., 2:, 1:-1] + padded[..., :-2, 1:-1] + padded[..., 1:-1, 2:] + padded[..., 1:-1, :-2] - 4.0 * values

def shot_sources(encodings, wavelet):
    columns = jnp.arange(NZ)
    spacing = NZ // NSHOT
    position = jnp.arange(NSHOT) * NZ // NSHOT + spacing // 2
    onehot = (position[:, None] == columns[None, :]).astype(jnp.float32)
    amplitude = encodings.astype(jnp.float32)[:, None, :] * wavelet[None, :, :]
    return jnp.einsum('stk,kz->stz', amplitude, onehot, precision=lax.Precision.HIGHEST)

def block_parity(row_index, bounds):
    inner = bounds[1:-1]
    return lax.optimization_barrier(jnp.sum((row_index[:, None] >= inner[None, :]).astype(jnp.int32), axis=1)) % 2

def forward_levels(pair, source_rows, coefficient):
    at_source = (jnp.arange(NX) == NX // 2).astype(jnp.float32)[:, None]
    before = pair[0]
    current = pair[1]
    history = [current]
    for moment in range(NT - 1):
        following = 2.0 * current - before + coefficient * laplace(current) + at_source * source_rows[moment][None, :]
        before, current = (current, following)
        history.append(current)
    return jnp.stack(history)

def increments(vectors, levels, coefficient, receiver):
    before = jnp.zeros_like(vectors)
    current = jnp.zeros_like(vectors)
    observed = []
    for moment in range(NT):
        following = 2.0 * current - before + coefficient * laplace(current) + vectors * levels[moment]
        before, current = (current, following)
        observed.append(receiver * following)
    return jnp.stack(observed)

def reference(probes, coarse_sample, coefficient, receiver, checkpoints, encodings, wavelet, bounds):
    parity = block_parity(jnp.arange(NX), bounds)
    colour = jnp.arange(PROBES) % 2
    support = (parity[None, :] == colour[:, None]).astype(jnp.float32)
    vectors = probes * support[:, :, None]
    sources = shot_sources(encodings, wavelet)

    def one_shot(accumulated, inputs):
        pair, source_rows = inputs
        levels = forward_levels(pair, source_rows, coefficient)

        def observe(moved):
            return increments(moved, levels, coefficient, receiver)
        observed, pullback = jax.vjp(observe, vectors)
        gradient, = pullback(observed)
        return (accumulated + gradient, None)
    hessian, _ = lax.scan(one_shot, jnp.zeros_like(vectors), (checkpoints, sources))
    keep = (parity[None, :] != colour[:, None]).astype(jnp.float32)
    return keep[:, :, None] * (hessian - coarse_sample)
```

```python
import functools
import jax
import jax.numpy as jnp
from jax import lax
from jax.experimental import pallas as pl
from jax.experimental.pallas import tpu as pltpu
from jax.sharding import PartitionSpec as P

NZ = 512
NSHOT = 256
CHUNK = 64
WIN = 80
EDGE = 8
LANES = 128
TILES = NZ // LANES
UNROLL = 4


def split(row):
    return [row[:, LANES * j : LANES * (j + 1)] for j in range(TILES)]


def sideways(tiles, first, last):
    right = [pltpu.roll(t, 1, 1) for t in tiles]
    left = [pltpu.roll(t, LANES - 1, 1) for t in tiles]
    zero = jnp.zeros_like(tiles[0])
    out = []
    for j in range(TILES):
        a = jnp.where(first, right[j - 1] if j else zero, right[j])
        b = jnp.where(last, left[j + 1] if j < TILES - 1 else zero, left[j])
        out.append(a + b)
    return out


def kernel(place, *refs, shots, has_total):
    slabs = refs[0:4]
    blocks = refs[4:8]
    parity_ref, coef_ref, recv_ref = refs[8:11]
    n = 11
    if has_total:
        totals = refs[n : n + 4]
        n += 4
    outs = refs[n : n + 4]
    u_ref, v_ref, e_ref, w_ref, grad_ref, *d_refs = refs[n + 4 :]
    d_refs = [d_refs[4 * i : 4 * i + 4] for i in range(shots)]

    lane = lax.broadcasted_iota(jnp.int32, (8, LANES), 1)
    first = lane == 0
    last = lane == LANES - 1

    for k in range(4):
        y = lax.rem(place[0] + k, 4)
        for i in range(shots):
            for lev in range(2):
                base = pl.multiple_of(EDGE + 16 * y, 8)
                u_ref[i, lev, pl.ds(base, 16), :] = slabs[k][i, lev, 0:16, :]

        @pl.when(y == 3)
        def _():
            for i in range(shots):
                for lev in range(2):
                    u_ref[i, lev, 0:8, :] = slabs[k][i, lev, 16:24, :]

        @pl.when(y == 0)
        def _():
            for i in range(shots):
                for lev in range(2):
                    u_ref[i, lev, 72:80, :] = slabs[k][i, lev, 16:24, :]
                for t in range(3):
                    u_ref[i, 5 + t // 2, 6 + t % 2 : 7 + t % 2, :] = slabs[k][
                        i, t // 2, 22 + t % 2 : 23 + t % 2, :
                    ]

    coef = coef_ref[...]
    e_ref[...] = 2.0 - 4.0 * coef
    w_ref[...] = recv_ref[...] * recv_ref[...]

    odd = parity_ref[...] > 0.5
    for q in range(4):
        w = blocks[q][...]
        for colour in range(2):
            v = jnp.where(odd if colour else jnp.logical_not(odd), w, 0.0)
            for j, tile in enumerate(split(v)):
                v_ref.at[j][pl.ds(2 * q + colour, WIN, stride=8), :] = tile

    row = lax.broadcasted_iota(jnp.int32, (WIN, NZ), 0)
    column = lax.broadcasted_iota(jnp.int32, (WIN, NZ), 1)
    at_source = row == place[1]
    for i in range(shots):
        for t in range(3):
            before = u_ref[i, t]
            now = u_ref[i, t + 1]
            up = pltpu.roll(now, 1, 0)
            down = pltpu.roll(now, WIN - 1, 0)
            right = jnp.where(column == 0, 0.0, pltpu.roll(now, 1, 1))
            left = jnp.where(column == NZ - 1, 0.0, pltpu.roll(now, NZ - 1, 1))
            amp = u_ref[i, 5 + t // 2, 6 + t % 2 : 7 + t % 2, :]
            after = (
                2.0 * now
                - before
                + coef * (up + down + left + right - 4.0 * now)
                + jnp.where(at_source, amp, 0.0)
            )
            u_ref[i, t + 2] = after

    def block(r):
        return pl.ds(pl.multiple_of(8 * r, 8), 8)

    def field(ref, r):
        return [ref[j, block(r), :] for j in range(TILES)]

    def wide(ref, r):
        return split(ref[pl.ds(r, 1), :])

    def store(ref, r, tiles):
        for j in range(TILES):
            ref[j, block(r), :] = tiles[j]

    def level(i, l, r):
        return split(u_ref[i, l + 1, pl.ds(r, 1), :])

    def start(r, _):
        v = field(v_ref, r)
        for i in range(shots):
            u = level(i, 0, r)
            store(d_refs[i][0], r, [a * b for a, b in zip(v, u)])
        return 0

    lax.fori_loop(2, 78, start, 0, unroll=UNROLL)

    def forward(t, r, carry):
        v = field(v_ref, r)
        c = wide(coef_ref, r)
        e = wide(e_ref, r)
        out = []
        for i in range(shots):
            up, mid = carry[2 * i], carry[2 * i + 1]
            down = field(d_refs[i][t - 1], r + 1)
            side = sideways(mid, first, last)
            u = level(i, t, r)
            new = []
            for j in range(TILES):
                x = e[j] * mid[j] + c[j] * (up[j] + down[j] + side[j]) + v[j] * u[j]
                new.append(x)
            if t >= 2:
                prev = field(d_refs[i][t - 2], r)
                new = [a - b for a, b in zip(new, prev)]
            store(d_refs[i][t], r, new)
            out += [mid, down]
        return out

    for t in range(1, 4):
        lo, hi = 2 + t, 78 - t
        init = []
        for i in range(shots):
            init += [field(d_refs[i][t - 1], lo - 1), field(d_refs[i][t - 1], lo)]
        lax.fori_loop(lo, hi, functools.partial(forward, t), init, unroll=UNROLL)

    def first_adjoint(r, _):
        w = wide(w_ref, r)
        for i in range(shots):
            d = field(d_refs[i][3], r)
            store(d_refs[i][3], r, [a * b for a, b in zip(w, d)])
        return 0

    lax.fori_loop(5, 75, first_adjoint, 0, unroll=UNROLL)

    def adjoint(t, r, carry):
        w = wide(w_ref, r)
        e = wide(e_ref, r)
        cn = wide(coef_ref, r + 1)
        out = []
        for i in range(shots):
            up, mid, here = carry[3 * i], carry[3 * i + 1], carry[3 * i + 2]
            below = field(d_refs[i][t + 1], r + 1)
            down = [a * b for a, b in zip(cn, below)]
            side = sideways(mid, first, last)
            d = field(d_refs[i][t], r)
            new = []
            for j in range(TILES):
                new.append(w[j] * d[j] + e[j] * here[j] + (up[j] + down[j] + side[j]))
            if t <= 1:
                beyond = field(d_refs[i][t + 2], r)
                new = [a - b for a, b in zip(new, beyond)]
            store(d_refs[i][t], r, new)
            out += [mid, down, below]
        return out

    for t in (2, 1, 0):
        lo, hi = 8 - t, 72 + t
        init = []
        c0, c1 = wide(coef_ref, lo - 1), wide(coef_ref, lo)
        for i in range(shots):
            a0, a1 = field(d_refs[i][t + 1], lo - 1), field(d_refs[i][t + 1], lo)
            init += [
                [a * b for a, b in zip(c0, a0)],
                [a * b for a, b in zip(c1, a1)],
                a1,
            ]
        lax.fori_loop(lo, hi, functools.partial(adjoint, t), init, unroll=UNROLL)

    def gather(r, _):
        total = None
        for i in range(shots):
            for t in range(4):
                a = field(d_refs[i][t], r)
                u = level(i, t, r)
                term = [p * q for p, q in zip(a, u)]
                total = term if total is None else [p + q for p, q in zip(total, term)]
        store(grad_ref, r - EDGE, total)
        return 0

    lax.fori_loop(EDGE, EDGE + CHUNK, gather, 0, unroll=UNROLL)

    odd = parity_ref[EDGE : EDGE + CHUNK, :] > 0.5
    for q in range(4):
        for j in range(TILES):
            here = slice(LANES * j, LANES * (j + 1))
            even = grad_ref.at[j][pl.ds(2 * q, CHUNK, stride=8), :]
            other = grad_ref.at[j][pl.ds(2 * q + 1, CHUNK, stride=8), :]
            result = jnp.where(odd[:, here], even, other)
            if has_total:
                result = result + totals[q][:, here]
            outs[q][:, here] = result


def apply(place, slabs, blocks, parity, coef, recv, totals=()):
    shots = slabs[0].shape[0]
    vm = pl.BlockSpec(memory_space=pltpu.VMEM)
    args = [*slabs, *blocks, parity, coef, recv, *totals]
    big = pltpu.VMEM((TILES, 8 * WIN, LANES), jnp.float32)
    return pl.pallas_call(
        functools.partial(kernel, shots=shots, has_total=bool(totals)),
        out_shape=[jax.ShapeDtypeStruct((CHUNK, NZ), jnp.float32)] * 4,
        in_specs=[pl.BlockSpec(memory_space=pltpu.SMEM)] + [vm] * len(args),
        out_specs=[vm] * 4,
        scratch_shapes=[
            pltpu.VMEM((shots, 7, WIN, NZ), jnp.float32),
            big,
            pltpu.VMEM((WIN, NZ), jnp.float32),
            pltpu.VMEM((WIN, NZ), jnp.float32),
            pltpu.VMEM((TILES, 8 * CHUNK, LANES), jnp.float32),
        ]
        + [big] * (4 * shots),
        compiler_params=pltpu.CompilerParams(vmem_limit_bytes=56 * 1024 * 1024),
        cost_estimate=pl.CostEstimate(
            flops=shots * 8 * 8 * 70 * 512 * 12, bytes_accessed=4 << 20, transcendentals=0
        ),
        name="hessian_rows",
    )(place, *args)


AXES = ("shot", "probe")


def index(x, zh, y, zl, c):
    return (zl * 2 + c) * 32 + x * 8 + zh * 4 + y


def routes(source_of):
    pairs = []
    for x in range(4):
        for zh in range(2):
            for y in range(4):
                for zl in range(4):
                    for c in range(2):
                        source = source_of(x, zh, y, zl, c)
                        if source is not None:
                            pairs.append((index(*source), index(x, zh, y, zl, c)))
    return pairs


def main_source(k, x, zh, y, zl, c):
    return zl, c, y, x, zh ^ k


def edge_source(k, x, zh, y, zl, c):
    chunk = zl * 2 + c + {0: 1, 3: -1}.get(y, 8)
    if chunk < 0 or chunk > 7:
        return None
    return chunk // 2, chunk % 2, y, x, zh ^ k


def along_y(k):
    return routes(lambda x, zh, y, zl, c: (x, zh, (y + k) % 4, zl, c))


def along_x(k):
    return routes(lambda x, zh, y, zl, c: ((x + k) % 4, zh, y, zl, c))


def shot_sources(encodings, wavelet):
    columns = jnp.arange(NZ)
    position = jnp.arange(NSHOT) * 2 + 1
    onehot = (position[:, None] == columns[None, :]).astype(jnp.float32)
    amplitude = encodings.astype(jnp.float32)[:, None, :] * wavelet[None, :, :]
    return jnp.einsum("stk,kz->stz", amplitude, onehot, precision=lax.Precision.HIGHEST)


def block_parity(row_index, bounds):
    inner = bounds[1:-1]
    return jnp.sum((row_index[:, None] >= inner[None, :]).astype(jnp.int32), axis=1) % 2


def window(array, chunk, dim):
    rows = array.shape[dim]
    top = lax.dynamic_slice_in_dim(array, jnp.maximum(chunk * CHUNK - EDGE, 0), EDGE, dim)
    mid = lax.dynamic_slice_in_dim(array, chunk * CHUNK, CHUNK, dim)
    low = lax.dynamic_slice_in_dim(
        array, jnp.minimum(chunk * CHUNK + CHUNK, rows - EDGE), EDGE, dim
    )
    return jnp.concatenate([top, mid, low], axis=dim)


def on_device(
    probes, coarse_sample, coefficient, receiver, checkpoints, encodings, wavelet, bounds
):
    chunk = lax.axis_index("shot")
    y = lax.axis_index("probe") % 4
    sources = shot_sources(encodings, wavelet)

    extra = jnp.concatenate([sources, jnp.zeros_like(sources[:, :1])], axis=1)
    extra = extra.reshape(2, 2, 2, NZ)
    below = jnp.concatenate([checkpoints[:, :, :6], extra], axis=2)
    edge = jnp.where(y == 0, below, checkpoints[:, :, 8:])

    slabs = []
    for k in range(2):
        main = lax.ppermute(checkpoints, AXES, routes(functools.partial(main_source, k)))
        side = lax.ppermute(edge, AXES, routes(functools.partial(edge_source, k)))
        own = jnp.concatenate([main, side], axis=2)
        slabs.append([own] + [lax.ppermute(own, AXES, along_y(d)) for d in (1, 2, 3)])

    row = chunk * CHUNK - EDGE + jnp.arange(WIN)
    inside = ((row >= 0) & (row < 512))[:, None]
    parity = block_parity(row, bounds)
    odd = (parity == 1)[:, None]
    pair = window(probes, chunk, 1)
    mine = jnp.where(inside, jnp.where(odd, pair[1], pair[0]), 0.0)
    blocks = [mine] + [lax.ppermute(mine, AXES, along_x(d)) for d in (1, 2, 3)]
    coef = jnp.where(inside, window(coefficient, chunk, 0), 0.0)
    recv = jnp.where(inside, window(receiver, chunk, 0), 0.0)
    colours = jnp.broadcast_to(odd.astype(jnp.float32), (WIN, NZ))
    place = jnp.stack([y, 256 - chunk * CHUNK + EDGE]).astype(jnp.int32)

    terms = apply(place, slabs[0], blocks, colours, coef, recv)
    terms = apply(place, slabs[1], blocks, colours, coef, recv, terms)
    total = terms[0]
    for d in (1, 2, 3):
        total = total + lax.ppermute(terms[d], AXES, along_x(4 - d))

    keep = odd[EDGE : EDGE + CHUNK]
    return jnp.stack(
        [
            jnp.where(keep, total - coarse_sample[0], 0.0),
            jnp.where(keep, 0.0, total - coarse_sample[1]),
        ]
    )


def solution(mesh):
    return jax.shard_map(
        on_device,
        mesh=mesh,
        in_specs=(
            P("probe", None, None),
            P("probe", "shot", None),
            P(),
            P(),
            P("shot", None, "probe", None),
            P("shot", None),
            P(),
            P(),
        ),
        out_specs=P("probe", "shot", None),
        check_vma=False,
    )
```

```python
import functools
import jax
import jax.numpy as jnp
from jax import lax
from jax.experimental import pallas as pl
from jax.experimental.pallas import tpu as pltpu
from jax.sharding import PartitionSpec as P

NZ = 512
NSHOT = 256
CHUNK = 64
WIN = 80
EDGE = 8
LANES = 128
TILES = NZ // LANES
UNROLLS = (74, 72, 70, 68, 66, 64)


def split(row):
    return [row[:, LANES * j : LANES * (j + 1)] for j in range(TILES)]


def sideways(tiles, first, last):
    left = jnp.where(first, 0.0, pltpu.roll(tiles[3], 1, 1))
    right = jnp.where(last, 0.0, pltpu.roll(tiles[0], LANES - 1, 1))
    return [left + tiles[1], tiles[0] + tiles[2], tiles[1] + tiles[3], tiles[2] + right]


def kernel(place, *refs, shots, has_total):
    slabs = refs[0:4]
    blocks = refs[4:8]
    parity_ref, coef_ref, recv_ref = refs[8:11]
    n = 11
    if has_total:
        totals = refs[n : n + 4]
        n += 4
    outs = refs[n : n + 4]
    u_ref, v_ref, e_ref, w_ref, grad_ref, *d_refs = refs[n + 4 :]
    d_refs = [d_refs[4 * i : 4 * i + 4] for i in range(shots)]

    lane = lax.broadcasted_iota(jnp.int32, (8, LANES), 1)
    first = lane == 0
    last = lane == LANES - 1

    for k in range(4):
        y = lax.rem(place[0] + k, 4)
        for i in range(shots):
            for lev in range(2):
                base = pl.multiple_of(EDGE + 16 * y, 8)
                u_ref[i, lev, pl.ds(base, 16), :] = slabs[k][i, lev, 0:16, :]

        @pl.when(y == 3)
        def _():
            for i in range(shots):
                for lev in range(2):
                    u_ref[i, lev, 0:8, :] = slabs[k][i, lev, 16:24, :]

        @pl.when(y == 0)
        def _():
            for i in range(shots):
                for lev in range(2):
                    u_ref[i, lev, 72:80, :] = slabs[k][i, lev, 16:24, :]
                for t in range(3):
                    u_ref[i, 5 + t // 2, 6 + t % 2 : 7 + t % 2, :] = slabs[k][
                        i, t // 2, 22 + t % 2 : 23 + t % 2, :
                    ]

    coef = coef_ref[...]
    e_ref[...] = 2.0 - 4.0 * coef
    w_ref[...] = recv_ref[...] * recv_ref[...]

    odd = parity_ref[...] > 0.5
    for q in range(4):
        w = blocks[q][...]
        for colour in range(2):
            v = jnp.where(odd if colour else jnp.logical_not(odd), w, 0.0)
            for j, tile in enumerate(split(v)):
                v_ref.at[j][pl.ds(2 * q + colour, WIN, stride=8), :] = tile

    row = lax.broadcasted_iota(jnp.int32, (WIN, LANES), 0)
    column = lax.broadcasted_iota(jnp.int32, (WIN, LANES), 1)
    at_source = row == place[1]
    for i in range(shots):
        for t in range(3):
            now = split(u_ref[i, t + 1])
            side = sideways(now, column == 0, column == LANES - 1)
            for j in range(TILES):
                here = slice(LANES * j, LANES * (j + 1))
                up = pltpu.roll(now[j], 1, 0)
                down = pltpu.roll(now[j], WIN - 1, 0)
                amp = u_ref[i, 5 + t // 2, 6 + t % 2 : 7 + t % 2, here]
                u_ref[i, t + 2, :, here] = (
                    e_ref[:, here] * now[j]
                    - u_ref[i, t, :, here]
                    + coef_ref[:, here] * (up + down + side[j])
                    + jnp.where(at_source, amp, 0.0)
                )

    def block(r):
        return pl.ds(pl.multiple_of(8 * r, 8), 8)

    def field(ref, r):
        return [ref[j, block(r), :] for j in range(TILES)]

    def wide(ref, r):
        return split(ref[pl.ds(r, 1), :])

    def store(ref, r, tiles):
        for j in range(TILES):
            ref[j, block(r), :] = tiles[j]

    def level(i, l, r):
        return split(u_ref[i, l + 1, pl.ds(r, 1), :])

    def times(a, b):
        return [p * q for p, q in zip(a, b)]

    def plus(a, b):
        return [p + q for p, q in zip(a, b)]

    def minus(a, b):
        return [p - q for p, q in zip(a, b)]

    def stencil(c, e, up, mid, down):
        side = sideways(mid, first, last)
        return plus(times(e, mid), times(c, plus(plus(up, down), side)))

    def source(i, r):
        return times(field(v_ref, r), level(i, 0, r))

    def forward(t, r, carry):
        v = field(v_ref, r)
        c = wide(coef_ref, r)
        e = wide(e_ref, r)
        w = wide(w_ref, r) if t == 3 else None
        ahead = field(v_ref, r + 1) if t == 1 else None
        out = []
        for i in range(shots):
            up, mid = carry[2 * i], carry[2 * i + 1]
            if t == 1:
                down = times(ahead, level(i, 0, r + 1))
                store(d_refs[i][0], r + 1, down)
            else:
                down = field(d_refs[i][t - 1], r + 1)
            new = plus(stencil(c, e, up, mid, down), times(v, level(i, t, r)))
            if t >= 2:
                new = minus(new, field(d_refs[i][t - 2], r))
            store(d_refs[i][t], r, times(w, new) if t == 3 else new)
            out += [mid, down]
        return out

    for t in range(1, 4):
        lo, hi = 2 + t, 78 - t
        init = []
        for i in range(shots):
            if t == 1:
                rows = [source(i, lo - 1), source(i, lo)]
                store(d_refs[i][0], lo, rows[1])
            else:
                rows = [field(d_refs[i][t - 1], lo - 1), field(d_refs[i][t - 1], lo)]
            init += rows
        lax.fori_loop(lo, hi, functools.partial(forward, t), init, unroll=UNROLLS[t - 1])

    def adjoint(t, r, carry):
        w = wide(w_ref, r)
        e = wide(e_ref, r)
        cn = wide(coef_ref, r + 1)
        out = []
        total = None
        for i in range(shots):
            up, mid, here = carry[3 * i], carry[3 * i + 1], carry[3 * i + 2]
            below = field(d_refs[i][t + 1], r + 1)
            down = times(cn, below)
            side = sideways(mid, first, last)
            new = plus(times(w, field(d_refs[i][t], r)), times(e, here))
            new = plus(new, plus(plus(up, down), side))
            if t <= 1:
                beyond = field(d_refs[i][t + 2], r)
                new = minus(new, beyond)
            if t == 0:
                final = field(d_refs[i][3], r)
                for l, a in enumerate((new, here, beyond, final)):
                    term = times(a, level(i, l, r))
                    total = term if total is None else plus(total, term)
            else:
                store(d_refs[i][t], r, new)
            out += [mid, down, below]
        if t == 0:
            store(grad_ref, r - EDGE, total)
        return out

    for t in (2, 1, 0):
        lo, hi = 8 - t, 72 + t
        init = []
        c0, c1 = wide(coef_ref, lo - 1), wide(coef_ref, lo)
        for i in range(shots):
            a0, a1 = field(d_refs[i][t + 1], lo - 1), field(d_refs[i][t + 1], lo)
            init += [times(c0, a0), times(c1, a1), a1]
        lax.fori_loop(lo, hi, functools.partial(adjoint, t), init, unroll=UNROLLS[5 - t])

    odd = parity_ref[EDGE : EDGE + CHUNK, :] > 0.5
    for q in range(4):
        for j in range(TILES):
            here = slice(LANES * j, LANES * (j + 1))
            even = grad_ref.at[j][pl.ds(2 * q, CHUNK, stride=8), :]
            other = grad_ref.at[j][pl.ds(2 * q + 1, CHUNK, stride=8), :]
            result = jnp.where(odd[:, here], even, other)
            if has_total:
                result = result + totals[q][:, here]
            outs[q][:, here] = result


def apply(place, slabs, blocks, parity, coef, recv, totals=()):
    shots = slabs[0].shape[0]
    vm = pl.BlockSpec(memory_space=pltpu.VMEM)
    args = [*slabs, *blocks, parity, coef, recv, *totals]
    big = pltpu.VMEM((TILES, 8 * WIN, LANES), jnp.float32)
    return pl.pallas_call(
        functools.partial(kernel, shots=shots, has_total=bool(totals)),
        out_shape=[jax.ShapeDtypeStruct((CHUNK, NZ), jnp.float32)] * 4,
        in_specs=[pl.BlockSpec(memory_space=pltpu.SMEM)] + [vm] * len(args),
        out_specs=[vm] * 4,
        scratch_shapes=[
            pltpu.VMEM((shots, 7, WIN, NZ), jnp.float32),
            big,
            pltpu.VMEM((WIN, NZ), jnp.float32),
            pltpu.VMEM((WIN, NZ), jnp.float32),
            pltpu.VMEM((TILES, 8 * CHUNK, LANES), jnp.float32),
        ]
        + [big] * (4 * shots),
        compiler_params=pltpu.CompilerParams(vmem_limit_bytes=56 * 1024 * 1024),
        cost_estimate=pl.CostEstimate(
            flops=shots * 8 * 8 * 70 * 512 * 12, bytes_accessed=4 << 20, transcendentals=0
        ),
        name="hessian_rows",
    )(place, *args)


AXES = ("shot", "probe")


def index(x, zh, y, zl, c):
    return (zl * 2 + c) * 32 + x * 8 + zh * 4 + y


def routes(source_of):
    pairs = []
    for x in range(4):
        for zh in range(2):
            for y in range(4):
                for zl in range(4):
                    for c in range(2):
                        source = source_of(x, zh, y, zl, c)
                        if source is not None:
                            pairs.append((index(*source), index(x, zh, y, zl, c)))
    return pairs


def main_source(k, x, zh, y, zl, c):
    return zl, c, y, x, zh ^ k


def edge_source(k, x, zh, y, zl, c):
    chunk = zl * 2 + c + {0: 1, 3: -1}.get(y, 8)
    if chunk < 0 or chunk > 7:
        return None
    return chunk // 2, chunk % 2, y, x, zh ^ k


def along_y(k):
    return routes(lambda x, zh, y, zl, c: (x, zh, (y + k) % 4, zl, c))


def along_x(k):
    return routes(lambda x, zh, y, zl, c: ((x + k) % 4, zh, y, zl, c))


def place_of(column):
    return column % TILES * LANES + column // TILES


def reorder(array, back=False):
    columns = jnp.arange(NZ)
    match = columns[None, :] == place_of(columns)[:, None]
    match = match.T if back else match
    return lax.dot_general(
        array,
        match.astype(jnp.float32),
        (((array.ndim - 1,), (0,)), ((), ())),
        precision=lax.Precision.HIGHEST,
    )


def shot_sources(encodings, wavelet):
    columns = jnp.arange(NZ)
    position = place_of(jnp.arange(NSHOT) * 2 + 1)
    onehot = (position[:, None] == columns[None, :]).astype(jnp.float32)
    amplitude = encodings.astype(jnp.float32)[:, None, :] * wavelet[None, :, :]
    return jnp.einsum("stk,kz->stz", amplitude, onehot, precision=lax.Precision.HIGHEST)


def block_parity(row_index, bounds):
    inner = bounds[1:-1]
    return jnp.sum((row_index[:, None] >= inner[None, :]).astype(jnp.int32), axis=1) % 2


def window(array, chunk, dim):
    rows = array.shape[dim]
    top = lax.dynamic_slice_in_dim(array, jnp.maximum(chunk * CHUNK - EDGE, 0), EDGE, dim)
    mid = lax.dynamic_slice_in_dim(array, chunk * CHUNK, CHUNK, dim)
    low = lax.dynamic_slice_in_dim(
        array, jnp.minimum(chunk * CHUNK + CHUNK, rows - EDGE), EDGE, dim
    )
    return jnp.concatenate([top, mid, low], axis=dim)


def on_device(
    probes, coarse_sample, coefficient, receiver, checkpoints, encodings, wavelet, bounds
):
    chunk = lax.axis_index("shot")
    y = lax.axis_index("probe") % 4
    sources = shot_sources(encodings, wavelet)
    checkpoints = reorder(checkpoints)

    row = chunk * CHUNK - EDGE + jnp.arange(WIN)
    inside = ((row >= 0) & (row < 512))[:, None]
    odd = (block_parity(row, bounds) == 1)[:, None]

    extra = jnp.concatenate([sources, jnp.zeros_like(sources[:, :1])], axis=1)
    extra = extra.reshape(2, 2, 2, NZ)
    below = jnp.concatenate([checkpoints[:, :, :6], extra], axis=2)
    edge = jnp.where(y == 0, below, checkpoints[:, :, 8:])
    checkpoints, edge = lax.optimization_barrier((checkpoints, edge))
    owns = []
    for k in range(2):
        main = lax.ppermute(checkpoints, AXES, routes(functools.partial(main_source, k)))
        side = lax.ppermute(edge, AXES, routes(functools.partial(edge_source, k)))
        owns.append(jnp.concatenate([main, side], axis=2))

    pair = window(probes, chunk, 1)
    mine = reorder(jnp.where(inside, jnp.where(odd, pair[1], pair[0]), 0.0))
    coef = reorder(jnp.where(inside, window(coefficient, chunk, 0), 0.0))
    recv = reorder(jnp.where(inside, window(receiver, chunk, 0), 0.0))
    colours = jnp.broadcast_to(odd.astype(jnp.float32), (WIN, NZ))
    place = jnp.stack([y, 256 - chunk * CHUNK + EDGE]).astype(jnp.int32)
    owns[0], mine, coef, recv, colours, place = lax.optimization_barrier(
        (owns[0], mine, coef, recv, colours, place)
    )

    slabs = [[own] + [lax.ppermute(own, AXES, along_y(d)) for d in (1, 2, 3)] for own in owns]
    blocks = [mine] + [lax.ppermute(mine, AXES, along_x(d)) for d in (1, 2, 3)]

    terms = apply(place, slabs[0], blocks, colours, coef, recv)
    terms = apply(place, slabs[1], blocks, colours, coef, recv, terms)
    total = terms[0]
    for d in (1, 2, 3):
        total = total + lax.ppermute(terms[d], AXES, along_x(4 - d))

    total = reorder(total, back=True)
    keep = odd[EDGE : EDGE + CHUNK]
    return jnp.stack(
        [
            jnp.where(keep, total - coarse_sample[0], 0.0),
            jnp.where(keep, 0.0, total - coarse_sample[1]),
        ]
    )


def solution(mesh):
    return jax.shard_map(
        on_device,
        mesh=mesh,
        in_specs=(
            P("probe", None, None),
            P("probe", "shot", None),
            P(),
            P(),
            P("shot", None, "probe", None),
            P("shot", None),
            P(),
            P(),
        ),
        out_specs=P("probe", "shot", None),
        check_vma=False,
    )
```

```python
import functools
import jax
import jax.numpy as jnp
from jax import lax
from jax.experimental import pallas as pl
from jax.experimental.pallas import tpu as pltpu
from jax.sharding import PartitionSpec as P

NZ = 512
NSHOT = 256
CHUNK = 64
WIN = 80
EDGE = 8
LANES = 128
TILES = NZ // LANES
UNROLLS = (74, 72, 70, 68, 66, 64)


def split(row):
    return [row[:, LANES * j : LANES * (j + 1)] for j in range(TILES)]


def sideways(tiles, first, last):
    left = jnp.where(first, 0.0, pltpu.roll(tiles[3], 1, 1))
    right = jnp.where(last, 0.0, pltpu.roll(tiles[0], LANES - 1, 1))
    return [left + tiles[1], tiles[0] + tiles[2], tiles[1] + tiles[3], tiles[2] + right]


def kernel(*refs, shots, has_total):
    my_y = lax.rem(lax.axis_index("probe"), 4)
    source_row = NZ // 2 + EDGE - CHUNK * lax.axis_index("shot")
    slabs = refs[0:4]
    blocks = refs[4:8]
    parity_ref, coef_ref, recv_ref = refs[8:11]
    n = 11
    if has_total:
        totals = refs[n : n + 4]
        n += 4
    outs = refs[n : n + 4]
    u_ref, v_ref, e_ref, w_ref, grad_ref, *d_refs = refs[n + 4 :]
    d_refs = [d_refs[4 * i : 4 * i + 4] for i in range(shots)]

    lane = lax.broadcasted_iota(jnp.int32, (8, LANES), 1)
    first = lane == 0
    last = lane == LANES - 1

    for k in range(4):
        y = lax.rem(my_y + k, 4)
        for i in range(shots):
            for lev in range(2):
                base = pl.multiple_of(EDGE + 16 * y, 8)
                u_ref[i, lev, pl.ds(base, 16), :] = slabs[k][i, lev, 0:16, :]

        @pl.when(y == 3)
        def _():
            for i in range(shots):
                for lev in range(2):
                    u_ref[i, lev, 0:8, :] = slabs[k][i, lev, 16:24, :]

        @pl.when(y == 0)
        def _():
            for i in range(shots):
                for lev in range(2):
                    u_ref[i, lev, 72:80, :] = slabs[k][i, lev, 16:24, :]
                for t in range(3):
                    u_ref[i, 5 + t // 2, 6 + t % 2 : 7 + t % 2, :] = slabs[k][
                        i, t // 2, 22 + t % 2 : 23 + t % 2, :
                    ]

    coef = coef_ref[...]
    e_ref[...] = 2.0 - 4.0 * coef
    w_ref[...] = recv_ref[...] * recv_ref[...]

    odd = parity_ref[...] > 0.5
    for q in range(4):
        w = blocks[q][...]
        for colour in range(2):
            v = jnp.where(odd if colour else jnp.logical_not(odd), w, 0.0)
            for j, tile in enumerate(split(v)):
                v_ref.at[j][pl.ds(2 * q + colour, WIN, stride=8), :] = tile

    row = lax.broadcasted_iota(jnp.int32, (WIN, LANES), 0)
    column = lax.broadcasted_iota(jnp.int32, (WIN, LANES), 1)
    at_source = row == source_row
    for i in range(shots):
        for t in range(3):
            now = split(u_ref[i, t + 1])
            side = sideways(now, column == 0, column == LANES - 1)
            for j in range(TILES):
                here = slice(LANES * j, LANES * (j + 1))
                up = pltpu.roll(now[j], 1, 0)
                down = pltpu.roll(now[j], WIN - 1, 0)
                amp = u_ref[i, 5 + t // 2, 6 + t % 2 : 7 + t % 2, here]
                u_ref[i, t + 2, :, here] = (
                    e_ref[:, here] * now[j]
                    - u_ref[i, t, :, here]
                    + coef_ref[:, here] * (up + down + side[j])
                    + jnp.where(at_source, amp, 0.0)
                )

    def block(r):
        return pl.ds(pl.multiple_of(8 * r, 8), 8)

    def field(ref, r):
        return [ref[j, block(r), :] for j in range(TILES)]

    def wide(ref, r):
        return split(ref[pl.ds(r, 1), :])

    def store(ref, r, tiles):
        for j in range(TILES):
            ref[j, block(r), :] = tiles[j]

    def level(i, l, r):
        return split(u_ref[i, l + 1, pl.ds(r, 1), :])

    def times(a, b):
        return [p * q for p, q in zip(a, b)]

    def plus(a, b):
        return [p + q for p, q in zip(a, b)]

    def minus(a, b):
        return [p - q for p, q in zip(a, b)]

    def stencil(c, e, up, mid, down):
        side = sideways(mid, first, last)
        return plus(times(e, mid), times(c, plus(plus(up, down), side)))

    def source(i, r):
        return times(field(v_ref, r), level(i, 0, r))

    def forward(t, r, carry):
        v = field(v_ref, r)
        c = wide(coef_ref, r)
        e = wide(e_ref, r)
        w = wide(w_ref, r) if t == 3 else None
        ahead = field(v_ref, r + 1) if t == 1 else None
        out = []
        for i in range(shots):
            up, mid = carry[2 * i], carry[2 * i + 1]
            if t == 1:
                down = times(ahead, level(i, 0, r + 1))
                store(d_refs[i][0], r + 1, down)
            else:
                down = field(d_refs[i][t - 1], r + 1)
            new = plus(stencil(c, e, up, mid, down), times(v, level(i, t, r)))
            if t >= 2:
                new = minus(new, field(d_refs[i][t - 2], r))
            store(d_refs[i][t], r, times(w, new) if t == 3 else new)
            out += [mid, down]
        return out

    for t in range(1, 4):
        lo, hi = 2 + t, 78 - t
        init = []
        for i in range(shots):
            if t == 1:
                rows = [source(i, lo - 1), source(i, lo)]
                store(d_refs[i][0], lo, rows[1])
            else:
                rows = [field(d_refs[i][t - 1], lo - 1), field(d_refs[i][t - 1], lo)]
            init += rows
        lax.fori_loop(lo, hi, functools.partial(forward, t), init, unroll=UNROLLS[t - 1])

    def adjoint(t, r, carry):
        w = wide(w_ref, r)
        e = wide(e_ref, r)
        cn = wide(coef_ref, r + 1)
        out = []
        total = None
        for i in range(shots):
            up, mid, here = carry[3 * i], carry[3 * i + 1], carry[3 * i + 2]
            below = field(d_refs[i][t + 1], r + 1)
            down = times(cn, below)
            side = sideways(mid, first, last)
            new = plus(times(w, field(d_refs[i][t], r)), times(e, here))
            new = plus(new, plus(plus(up, down), side))
            if t <= 1:
                beyond = field(d_refs[i][t + 2], r)
                new = minus(new, beyond)
            if t == 0:
                final = field(d_refs[i][3], r)
                for l, a in enumerate((new, here, beyond, final)):
                    term = times(a, level(i, l, r))
                    total = term if total is None else plus(total, term)
            else:
                store(d_refs[i][t], r, new)
            out += [mid, down, below]
        if t == 0:
            store(grad_ref, r - EDGE, total)
        return out

    for t in (2, 1, 0):
        lo, hi = 8 - t, 72 + t
        init = []
        c0, c1 = wide(coef_ref, lo - 1), wide(coef_ref, lo)
        for i in range(shots):
            a0, a1 = field(d_refs[i][t + 1], lo - 1), field(d_refs[i][t + 1], lo)
            init += [times(c0, a0), times(c1, a1), a1]
        lax.fori_loop(lo, hi, functools.partial(adjoint, t), init, unroll=UNROLLS[5 - t])

    odd = parity_ref[EDGE : EDGE + CHUNK, :] > 0.5
    for q in range(4):
        for j in range(TILES):
            here = slice(LANES * j, LANES * (j + 1))
            even = grad_ref.at[j][pl.ds(2 * q, CHUNK, stride=8), :]
            other = grad_ref.at[j][pl.ds(2 * q + 1, CHUNK, stride=8), :]
            result = jnp.where(odd[:, here], even, other)
            if has_total:
                result = result + totals[q][:, here]
            outs[q][:, here] = result


def apply(slabs, blocks, parity, coef, recv, totals=()):
    shots = slabs[0].shape[0]
    vm = pl.BlockSpec(memory_space=pltpu.VMEM)
    args = [*slabs, *blocks, parity, coef, recv, *totals]
    big = pltpu.VMEM((TILES, 8 * WIN, LANES), jnp.float32)
    return pl.pallas_call(
        functools.partial(kernel, shots=shots, has_total=bool(totals)),
        out_shape=[jax.ShapeDtypeStruct((CHUNK, NZ), jnp.float32)] * 4,
        in_specs=[vm] * len(args),
        out_specs=[vm] * 4,
        scratch_shapes=[
            pltpu.VMEM((shots, 7, WIN, NZ), jnp.float32),
            big,
            pltpu.VMEM((WIN, NZ), jnp.float32),
            pltpu.VMEM((WIN, NZ), jnp.float32),
            pltpu.VMEM((TILES, 8 * CHUNK, LANES), jnp.float32),
        ]
        + [big] * (4 * shots),
        compiler_params=pltpu.CompilerParams(vmem_limit_bytes=56 * 1024 * 1024),
        cost_estimate=pl.CostEstimate(
            flops=shots * 8 * 8 * 70 * 512 * 12, bytes_accessed=4 << 20, transcendentals=0
        ),
        name="hessian_rows",
    )(*args)


def match(sources, column_of):
    shape = (sources, NZ)
    column = column_of(lax.broadcasted_iota(jnp.int32, shape, 0))
    place = lax.broadcasted_iota(jnp.int32, shape, 1)
    kept = TILES * (place & (LANES - 1)) + place // LANES
    return jnp.where(column == kept, 1.0, 0.0).astype(jnp.float32)


def exact_dot(a, b, transposed=False):
    dims = (((1,), (1 if transposed else 0,)), ((), ()))
    return lax.dot_general(
        a, b, dims, precision=lax.Precision.HIGHEST, preferred_element_type=jnp.float32
    )


def emit_kernel(levels_ref, enc_ref, wav_ref, main_ref, edge_ref):
    y = lax.rem(lax.axis_index("probe"), 4)
    moved = exact_dot(levels_ref[...].reshape(64, NZ), match(NZ, lambda c: c))
    main_ref[...] = moved.reshape(2, 2, 16, NZ)
    signs = enc_ref[...].astype(jnp.float32)
    rows = [signs[i : i + 1] * wav_ref[t : t + 1, :] for i in range(2) for t in range(3)]
    rows += [jnp.zeros_like(rows[0])] * 2
    amps = exact_dot(jnp.concatenate(rows, axis=0), match(NSHOT, lambda k: 2 * k + 1))
    lowest = y == 0
    for i in range(2):
        for lev in range(2):
            base = 16 * (2 * i + lev)
            edge_ref[i, lev] = jnp.where(lowest, moved[base : base + 8], moved[base + 8 : base + 16])

    @pl.when(lowest)
    def _():
        for i in range(2):
            for t in range(3):
                row = 6 + t % 2
                edge_ref[i, t // 2, row : row + 1, :] = amps[3 * i + t : 3 * i + t + 1]


def emit(levels, encodings, wavelet):
    vm = pl.BlockSpec(memory_space=pltpu.VMEM)
    return pl.pallas_call(
        emit_kernel,
        out_shape=[
            jax.ShapeDtypeStruct((2, 2, 16, NZ), jnp.float32),
            jax.ShapeDtypeStruct((2, 2, 8, NZ), jnp.float32),
        ],
        in_specs=[vm] * 3,
        out_specs=[vm] * 2,
        name="own_rows",
    )(levels, encodings, wavelet)


def prepare_kernel(bounds_ref, probes, coefficient, receiver, *refs):
    mine_ref, coef_ref, recv_ref, colour_ref, pair, coef, recv, sem = refs
    chunk = lax.axis_index("shot")
    first = pl.multiple_of(chunk * CHUNK, 8)
    above = pl.multiple_of(jnp.maximum(first - EDGE, 0), 8)
    below = pl.multiple_of(jnp.minimum(first + CHUNK, NZ - EDGE), 8)
    copies = []
    for start, at, size in ((above, 0, EDGE), (first, EDGE, CHUNK), (below, EDGE + CHUNK, EDGE)):
        rows, spot = pl.ds(start, size), pl.ds(at, size)
        for source, target in (
            (probes.at[:, rows, :], pair.at[:, spot, :]),
            (coefficient.at[rows, :], coef.at[spot, :]),
            (receiver.at[rows, :], recv.at[spot, :]),
        ):
            copy = pltpu.make_async_copy(source, target, sem.at[len(copies)])
            copy.start()
            copies.append(copy)
    order = match(NZ, lambda c: c)
    row = chunk * CHUNK - EDGE + lax.broadcasted_iota(jnp.int32, (WIN, 65), 0)
    lane = lax.broadcasted_iota(jnp.int32, (WIN, 65), 1)
    counted = (row >= bounds_ref[...]) & (lane >= 1) & (lane <= 63)
    block = jnp.sum(jnp.where(counted, 1.0, 0.0), axis=1, keepdims=True)
    odd = block - 2.0 * jnp.floor(0.5 * block)
    odd = jnp.broadcast_to(odd, (WIN, NZ))
    colour_ref[...] = odd
    row = chunk * CHUNK - EDGE + lax.broadcasted_iota(jnp.int32, (WIN, NZ), 0)
    inside = (row >= 0) & (row < NZ)
    for copy in copies:
        copy.wait()
    mine = jnp.where(odd > 0.5, pair[1], pair[0])
    for value, out in ((mine, mine_ref), (coef[...], coef_ref), (recv[...], recv_ref)):
        out[...] = exact_dot(jnp.where(inside, value, 0.0), order)


def prepare(bounds, probes, coefficient, receiver):
    vm = pl.BlockSpec(memory_space=pltpu.VMEM)
    hbm = pl.BlockSpec(memory_space=pl.ANY)
    field = pltpu.VMEM((WIN, NZ), jnp.float32)
    return pl.pallas_call(
        prepare_kernel,
        out_shape=[jax.ShapeDtypeStruct((WIN, NZ), jnp.float32)] * 4,
        in_specs=[vm, hbm, hbm, hbm],
        out_specs=[vm] * 4,
        scratch_shapes=[
            pltpu.VMEM((2, WIN, NZ), jnp.float32),
            field,
            field,
            pltpu.SemaphoreType.DMA((9,)),
        ],
        cost_estimate=pl.CostEstimate(flops=0, bytes_accessed=12 << 20, transcendentals=0),
        name="own_windows",
    )(bounds, probes, coefficient, receiver)


def finish_kernel(a, b, c, d, colour, coarse, out):
    total = exact_dot(a[...] + b[...] + c[...] + d[...], match(NZ, lambda c: c), transposed=True)
    odd = colour[EDGE : EDGE + CHUNK, :] > 0.5
    out[0] = jnp.where(odd, total - coarse[0], 0.0)
    out[1] = jnp.where(odd, 0.0, total - coarse[1])


def finish(terms, colour, coarse):
    vm = pl.BlockSpec(memory_space=pltpu.VMEM)
    return pl.pallas_call(
        finish_kernel,
        out_shape=jax.ShapeDtypeStruct((2, CHUNK, NZ), jnp.float32),
        in_specs=[vm] * 6,
        out_specs=vm,
        name="samples",
    )(*terms, colour, coarse)


AXES = ("shot", "probe")


def index(x, zh, y, zl, c):
    return (zl * 2 + c) * 32 + x * 8 + zh * 4 + y


def routes(source_of):
    pairs = []
    for x in range(4):
        for zh in range(2):
            for y in range(4):
                for zl in range(4):
                    for c in range(2):
                        source = source_of(x, zh, y, zl, c)
                        if source is not None:
                            pairs.append((index(*source), index(x, zh, y, zl, c)))
    return pairs


def main_source(k, x, zh, y, zl, c):
    return zl, c, y, x, zh ^ k


def edge_source(k, x, zh, y, zl, c):
    chunk = zl * 2 + c + {0: 1, 3: -1}.get(y, 8)
    if chunk < 0 or chunk > 7:
        return None
    return chunk // 2, chunk % 2, y, x, zh ^ k


def along_y(k):
    return routes(lambda x, zh, y, zl, c: (x, zh, (y + k) % 4, zl, c))


def along_x(k):
    return routes(lambda x, zh, y, zl, c: ((x + k) % 4, zh, y, zl, c))


def on_device(
    probes, coarse_sample, coefficient, receiver, checkpoints, encodings, wavelet, bounds
):
    levels, edge = emit(checkpoints, encodings, wavelet)
    owns = []
    for k in range(2):
        main = lax.ppermute(levels, AXES, routes(functools.partial(main_source, k)))
        side = lax.ppermute(edge, AXES, routes(functools.partial(edge_source, k)))
        owns.append(jnp.concatenate([main, side], axis=2))

    mine, coef, recv, colours = prepare(
        bounds.reshape(1, 65), probes, coefficient, receiver
    )
    owns[1], mine, coef, recv, colours = lax.optimization_barrier(
        (owns[1], mine, coef, recv, colours)
    )

    slabs = [[own] + [lax.ppermute(own, AXES, along_y(d)) for d in (1, 2, 3)] for own in owns]
    blocks = [mine] + [lax.ppermute(mine, AXES, along_x(d)) for d in (1, 2, 3)]

    terms = apply(slabs[0], blocks, colours, coef, recv)
    terms = apply(slabs[1], blocks, colours, coef, recv, terms)
    parts = [terms[0]] + [lax.ppermute(terms[d], AXES, along_x(4 - d)) for d in (1, 2, 3)]
    return finish(parts, colours, coarse_sample)


def solution(mesh):
    return jax.shard_map(
        on_device,
        mesh=mesh,
        in_specs=(
            P("probe", None, None),
            P("probe", "shot", None),
            P(),
            P(),
            P("shot", None, "probe", None),
            P("shot", None),
            P(),
            P(),
        ),
        out_specs=P("probe", "shot", None),
        check_vma=False,
    )
```

```python
import functools
import jax
import jax.numpy as jnp
from jax import lax
from jax.experimental import pallas as pl
from jax.experimental.pallas import tpu as pltpu
from jax.sharding import PartitionSpec as P

NZ = 512
NSHOT = 256
CHUNK = 64
WIN = 80
EDGE = 8
LANES = 128
TILES = NZ // LANES
UNROLLS = (74, 72, 70, 68, 66, 64)


def split(row):
    return [row[:, LANES * j : LANES * (j + 1)] for j in range(TILES)]


def sideways(tiles, first, last):
    left = jnp.where(first, 0.0, pltpu.roll(tiles[3], 1, 1))
    right = jnp.where(last, 0.0, pltpu.roll(tiles[0], LANES - 1, 1))
    return [left + tiles[1], tiles[0] + tiles[2], tiles[1] + tiles[3], tiles[2] + right]


def kernel(*refs, shots):
    my_y = lax.rem(lax.axis_index("probe"), 4)
    source_row = NZ // 2 + EDGE - CHUNK * lax.axis_index("shot")
    slabs = refs[0:4]
    blocks = refs[4:8]
    parity_ref, coef_ref, recv_ref = refs[8:11]
    n = 11
    outs = refs[n : n + 4]
    u_ref, edge_ref, sem, v_ref, e_ref, w_ref, grad_ref, back_ref, *d_refs = refs[n + 4 :]
    d_refs = [d_refs[4 * i : 4 * i + 4] for i in range(2)]

    lane = lax.broadcasted_iota(jnp.int32, (8, LANES), 1)
    first = lane == 0
    last = lane == LANES - 1

    copies = []
    for k in range(4):
        base = pl.multiple_of(EDGE + 16 * lax.rem(my_y + k, 4), 8)
        for source, target in (
            (slabs[k].at[:, :, 0:16, :], u_ref.at[:, 0:2, pl.ds(base, 16), :]),
            (slabs[k].at[:, :, 16:24, :], edge_ref.at[k]),
        ):
            copies.append(pltpu.make_async_copy(source, target, sem.at[len(copies)]))
            copies[-1].start()

    back_ref[...] = match(NZ, None, back=True)
    coef = coef_ref[...]
    e_ref[...] = 2.0 - 4.0 * coef
    w_ref[...] = recv_ref[...] * recv_ref[...]

    odd = parity_ref[...] > 0.5
    for q in range(4):
        w = blocks[q][...]
        for colour in range(2):
            v = jnp.where(odd if colour else jnp.logical_not(odd), w, 0.0)
            for j, tile in enumerate(split(v)):
                v_ref.at[j][pl.ds(2 * q + colour, WIN, stride=8), :] = tile

    for copy in copies:
        copy.wait()
    for k in range(4):
        y = lax.rem(my_y + k, 4)

        @pl.when(y == 3)
        def _():
            u_ref[:, 0:2, 0:8, :] = edge_ref[k]

        @pl.when(y == 0)
        def _():
            u_ref[:, 0:2, 72:80, :] = edge_ref[k]
            u_ref[:, 5:7, 6:8, :] = edge_ref[k, :, :, 6:8, :]

    row = lax.broadcasted_iota(jnp.int32, (WIN, LANES), 0)
    column = lax.broadcasted_iota(jnp.int32, (WIN, LANES), 1)
    at_source = row == source_row
    for i in range(shots):
        for t in range(3):
            now = split(u_ref[i, t + 1])
            side = sideways(now, column == 0, column == LANES - 1)
            for j in range(TILES):
                here = slice(LANES * j, LANES * (j + 1))
                up = pltpu.roll(now[j], 1, 0)
                down = pltpu.roll(now[j], WIN - 1, 0)
                amp = u_ref[i, 5 + t // 2, 6 + t % 2 : 7 + t % 2, here]
                u_ref[i, t + 2, :, here] = (
                    e_ref[:, here] * now[j]
                    - u_ref[i, t, :, here]
                    + coef_ref[:, here] * (up + down + side[j])
                    + jnp.where(at_source, amp, 0.0)
                )

    def block(r):
        return pl.ds(pl.multiple_of(8 * r, 8), 8)

    def field(ref, r):
        return [ref[j, block(r), :] for j in range(TILES)]

    def wide(ref, r):
        return split(ref[pl.ds(r, 1), :])

    def store(ref, r, tiles):
        for j in range(TILES):
            ref[j, block(r), :] = tiles[j]

    def level(i, l, r):
        return split(u_ref[i, l + 1, pl.ds(r, 1), :])

    def times(a, b):
        return [p * q for p, q in zip(a, b)]

    def plus(a, b):
        return [p + q for p, q in zip(a, b)]

    def minus(a, b):
        return [p - q for p, q in zip(a, b)]

    def stencil(c, e, up, mid, down):
        side = sideways(mid, first, last)
        return plus(times(e, mid), times(c, plus(plus(up, down), side)))

    def sweeps(group):
        def source(i, r):
            return times(field(v_ref, r), level(2 * group + i, 0, r))

        def forward(t, r, carry):
            v = field(v_ref, r)
            c = wide(coef_ref, r)
            e = wide(e_ref, r)
            w = wide(w_ref, r) if t == 3 else None
            ahead = field(v_ref, r + 1) if t == 1 else None
            out = []
            for i in range(2):
                up, mid = carry[2 * i], carry[2 * i + 1]
                if t == 1:
                    down = times(ahead, level(2 * group + i, 0, r + 1))
                    store(d_refs[i][0], r + 1, down)
                else:
                    down = field(d_refs[i][t - 1], r + 1)
                new = plus(stencil(c, e, up, mid, down), times(v, level(2 * group + i, t, r)))
                if t >= 2:
                    new = minus(new, field(d_refs[i][t - 2], r))
                store(d_refs[i][t], r, times(w, new) if t == 3 else new)
                out += [mid, down]
            return out

        for t in range(1, 4):
            lo, hi = 2 + t, 78 - t
            init = []
            for i in range(2):
                if t == 1:
                    rows = [source(i, lo - 1), source(i, lo)]
                    store(d_refs[i][0], lo, rows[1])
                else:
                    rows = [field(d_refs[i][t - 1], lo - 1), field(d_refs[i][t - 1], lo)]
                init += rows
            lax.fori_loop(lo, hi, functools.partial(forward, t), init, unroll=UNROLLS[t - 1])

        def adjoint(t, r, carry):
            w = wide(w_ref, r)
            e = wide(e_ref, r)
            cn = wide(coef_ref, r + 1)
            out = []
            total = None
            for i in range(2):
                up, mid, here = carry[3 * i], carry[3 * i + 1], carry[3 * i + 2]
                below = field(d_refs[i][t + 1], r + 1)
                down = times(cn, below)
                side = sideways(mid, first, last)
                new = plus(times(w, field(d_refs[i][t], r)), times(e, here))
                new = plus(new, plus(plus(up, down), side))
                if t <= 1:
                    beyond = field(d_refs[i][t + 2], r)
                    new = minus(new, beyond)
                if t == 0:
                    final = field(d_refs[i][3], r)
                    for l, a in enumerate((new, here, beyond, final)):
                        term = times(a, level(2 * group + i, l, r))
                        total = term if total is None else plus(total, term)
                else:
                    store(d_refs[i][t], r, new)
                out += [mid, down, below]
            if t == 0:
                if group:
                    total = plus(total, field(grad_ref, r - EDGE))
                store(grad_ref, r - EDGE, total)
            return out

        for t in (2, 1, 0):
            lo, hi = 8 - t, 72 + t
            init = []
            c0, c1 = wide(coef_ref, lo - 1), wide(coef_ref, lo)
            for i in range(2):
                a0, a1 = field(d_refs[i][t + 1], lo - 1), field(d_refs[i][t + 1], lo)
                init += [times(c0, a0), times(c1, a1), a1]
            lax.fori_loop(lo, hi, functools.partial(adjoint, t), init, unroll=UNROLLS[5 - t])

    for group in range(shots // 2):
        sweeps(group)

    odd = parity_ref[EDGE : EDGE + CHUNK, :] > 0.5
    rows = []
    for q in range(4):
        tiles = []
        for j in range(TILES):
            even = grad_ref.at[j][pl.ds(2 * q, CHUNK, stride=8), :]
            other = grad_ref.at[j][pl.ds(2 * q + 1, CHUNK, stride=8), :]
            tiles.append(jnp.where(odd[:, LANES * j : LANES * (j + 1)], even, other))
        rows.append(jnp.concatenate(tiles, axis=1))
    result = exact_dot(jnp.concatenate(rows, axis=0), back_ref[...])
    for q in range(4):
        outs[q][...] = result[CHUNK * q : CHUNK * (q + 1)]


def apply(slabs, blocks, parity, coef, recv):
    shots = slabs[0].shape[0]
    vm = pl.BlockSpec(memory_space=pltpu.VMEM)
    args = [*slabs, *blocks, parity, coef, recv]
    big = pltpu.VMEM((TILES, 8 * WIN, LANES), jnp.float32)
    return pl.pallas_call(
        functools.partial(kernel, shots=shots),
        out_shape=[jax.ShapeDtypeStruct((CHUNK, NZ), jnp.float32)] * 4,
        in_specs=[pl.BlockSpec(memory_space=pltpu.HBM)] * 4 + [vm] * (len(args) - 4),
        out_specs=[vm] * 4,
        scratch_shapes=[
            pltpu.VMEM((shots, 7, WIN, NZ), jnp.float32),
            pltpu.VMEM((4, shots, 2, 8, NZ), jnp.float32),
            pltpu.SemaphoreType.DMA((8,)),
            big,
            pltpu.VMEM((WIN, NZ), jnp.float32),
            pltpu.VMEM((WIN, NZ), jnp.float32),
            pltpu.VMEM((TILES, 8 * CHUNK, LANES), jnp.float32),
            pltpu.VMEM((NZ, NZ), jnp.bfloat16),
        ]
        + [big] * 8,
        compiler_params=pltpu.CompilerParams(vmem_limit_bytes=56 * 1024 * 1024),
        cost_estimate=pl.CostEstimate(
            flops=shots * 8 * 8 * 70 * 512 * 12, bytes_accessed=4 << 20, transcendentals=0
        ),
        name="hessian_rows",
    )(*args)


def match(sources, column_of, back=False):
    shape = (sources, NZ)
    here = lax.broadcasted_iota(jnp.int32, shape, 0)
    there = lax.broadcasted_iota(jnp.int32, shape, 1)
    place, column = (here, there) if back else (there, column_of(here))
    kept = TILES * (place & (LANES - 1)) + (place >> 7)
    return jnp.where(column == kept, 1.0, 0.0).astype(jnp.bfloat16)


def exact_dot(a, b):
    high = a.astype(jnp.bfloat16)
    rest = a - high.astype(jnp.float32)
    middle = rest.astype(jnp.bfloat16)
    low = (rest - middle.astype(jnp.float32)).astype(jnp.bfloat16)
    x, y, z = (jnp.dot(part, b, preferred_element_type=jnp.float32) for part in (high, middle, low))
    return x + y + z


def emit_kernel(levels_ref, enc_ref, wav_ref, main_ref, edge_ref):
    y = lax.rem(lax.axis_index("probe"), 4)
    moved = exact_dot(levels_ref[...].reshape(64, NZ), match(NZ, lambda c: c))
    main_ref[...] = moved.reshape(2, 2, 16, NZ)
    signs = enc_ref[...].astype(jnp.float32)
    rows = [signs[i : i + 1] * wav_ref[t : t + 1, :] for i in range(2) for t in range(3)]
    rows += [jnp.zeros_like(rows[0])] * 2
    amps = exact_dot(jnp.concatenate(rows, axis=0), match(NSHOT, lambda k: 2 * k + 1))
    lowest = y == 0
    for i in range(2):
        for lev in range(2):
            base = 16 * (2 * i + lev)
            edge_ref[i, lev] = jnp.where(lowest, moved[base : base + 8], moved[base + 8 : base + 16])

    @pl.when(lowest)
    def _():
        for i in range(2):
            for t in range(3):
                row = 6 + t % 2
                edge_ref[i, t // 2, row : row + 1, :] = amps[3 * i + t : 3 * i + t + 1]


def emit(levels, encodings, wavelet):
    vm = pl.BlockSpec(memory_space=pltpu.VMEM)
    return pl.pallas_call(
        emit_kernel,
        out_shape=[
            jax.ShapeDtypeStruct((2, 2, 16, NZ), jnp.float32),
            jax.ShapeDtypeStruct((2, 2, 8, NZ), jnp.float32),
        ],
        in_specs=[vm] * 3,
        out_specs=[vm] * 2,
        name="own_rows",
    )(levels, encodings, wavelet)


def prepare_kernel(bounds_ref, probes, coefficient, receiver, *refs):
    mine_ref, coef_ref, recv_ref, colour_ref, pair, coef, recv, sem = refs
    chunk = lax.axis_index("shot")
    first = pl.multiple_of(chunk * CHUNK, 8)
    above = pl.multiple_of(jnp.maximum(first - EDGE, 0), 8)
    below = pl.multiple_of(jnp.minimum(first + CHUNK, NZ - EDGE), 8)
    copies = []
    for start, at, size in ((above, 0, EDGE), (first, EDGE, CHUNK), (below, EDGE + CHUNK, EDGE)):
        rows, spot = pl.ds(start, size), pl.ds(at, size)
        for source, target in (
            (probes.at[:, rows, :], pair.at[:, spot, :]),
            (coefficient.at[rows, :], coef.at[spot, :]),
            (receiver.at[rows, :], recv.at[spot, :]),
        ):
            copy = pltpu.make_async_copy(source, target, sem.at[len(copies)])
            copy.start()
            copies.append(copy)
    order = match(NZ, lambda c: c)
    row = chunk * CHUNK - EDGE + lax.broadcasted_iota(jnp.int32, (WIN, 65), 0)
    lane = lax.broadcasted_iota(jnp.int32, (WIN, 65), 1)
    counted = (row >= bounds_ref[...]) & (lane >= 1) & (lane <= 63)
    block = jnp.sum(jnp.where(counted, 1.0, 0.0), axis=1, keepdims=True)
    odd = block - 2.0 * jnp.floor(0.5 * block)
    odd = jnp.broadcast_to(odd, (WIN, NZ))
    colour_ref[...] = odd
    row = chunk * CHUNK - EDGE + lax.broadcasted_iota(jnp.int32, (WIN, NZ), 0)
    inside = (row >= 0) & (row < NZ)
    for copy in copies:
        copy.wait()
    mine = jnp.where(odd > 0.5, pair[1], pair[0])
    for value, out in ((mine, mine_ref), (coef[...], coef_ref), (recv[...], recv_ref)):
        out[...] = exact_dot(jnp.where(inside, value, 0.0), order)


def prepare(bounds, probes, coefficient, receiver):
    vm = pl.BlockSpec(memory_space=pltpu.VMEM)
    hbm = pl.BlockSpec(memory_space=pl.ANY)
    field = pltpu.VMEM((WIN, NZ), jnp.float32)
    return pl.pallas_call(
        prepare_kernel,
        out_shape=[jax.ShapeDtypeStruct((WIN, NZ), jnp.float32)] * 4,
        in_specs=[vm, hbm, hbm, hbm],
        out_specs=[vm] * 4,
        scratch_shapes=[
            pltpu.VMEM((2, WIN, NZ), jnp.float32),
            field,
            field,
            pltpu.SemaphoreType.DMA((9,)),
        ],
        cost_estimate=pl.CostEstimate(flops=0, bytes_accessed=12 << 20, transcendentals=0),
        name="own_windows",
    )(bounds, probes, coefficient, receiver)


AXES = ("shot", "probe")


def index(x, zh, y, zl, c):
    return (zl * 2 + c) * 32 + x * 8 + zh * 4 + y


def routes(source_of):
    pairs = []
    for x in range(4):
        for zh in range(2):
            for y in range(4):
                for zl in range(4):
                    for c in range(2):
                        source = source_of(x, zh, y, zl, c)
                        if source is not None:
                            pairs.append((index(*source), index(x, zh, y, zl, c)))
    return pairs


def main_source(k, x, zh, y, zl, c):
    return zl, c, y, x, zh ^ k


def edge_source(k, x, zh, y, zl, c):
    chunk = zl * 2 + c + {0: 1, 3: -1}.get(y, 8)
    if chunk < 0 or chunk > 7:
        return None
    return chunk // 2, chunk % 2, y, x, zh ^ k


def along_y(k):
    return routes(lambda x, zh, y, zl, c: (x, zh, (y + k) % 4, zl, c))


def along_x(k):
    return routes(lambda x, zh, y, zl, c: ((x + k) % 4, zh, y, zl, c))


def spread(array, along):
    far = lax.ppermute(array, AXES, along(2))
    return [array, lax.ppermute(array, AXES, along(1)), far, lax.ppermute(array, AXES, along(3))]


def on_device(
    probes, coarse_sample, coefficient, receiver, checkpoints, encodings, wavelet, bounds
):
    levels, edge = emit(checkpoints, encodings, wavelet)
    owns = []
    for k in range(2):
        main = lax.ppermute(levels, AXES, routes(functools.partial(main_source, k)))
        side = lax.ppermute(edge, AXES, routes(functools.partial(edge_source, k)))
        owns.append(jnp.concatenate([main, side], axis=2))

    mine, coef, recv, colours = prepare(
        bounds.reshape(1, 65), probes, coefficient, receiver
    )

    own, mine, coef, recv, colours = lax.optimization_barrier(
        (jnp.concatenate(owns, axis=0), mine, coef, recv, colours)
    )
    slabs = spread(own, along_y)
    blocks = spread(mine, along_x)

    terms = apply(slabs, blocks, colours, coef, recv)
    parts = [terms[0]] + [lax.ppermute(terms[d], AXES, along_x(4 - d)) for d in (2, 1, 3)]
    total = parts[0] + parts[1] + parts[2] + parts[3]
    odd = colours[EDGE : EDGE + CHUNK] > 0.5
    keep = odd[None] != (jnp.arange(2) == 1)[:, None, None]
    return jnp.where(keep, total[None] - coarse_sample, 0.0)


def solution(mesh):
    return jax.shard_map(
        on_device,
        mesh=mesh,
        in_specs=(
            P("probe", None, None),
            P("probe", "shot", None),
            P(),
            P(),
            P("shot", None, "probe", None),
            P("shot", None),
            P(),
            P(),
        ),
        out_specs=P("probe", "shot", None),
        check_vma=False,
    )
```

```python
import functools
import jax
import jax.numpy as jnp
from jax import lax
from jax.experimental import pallas as pl
from jax.experimental.pallas import tpu as pltpu
from jax.sharding import PartitionSpec as P

NZ = 512
NSHOT = 256
CHUNK = 64
WIN = 80
EDGE = 8
LANES = 128
TILES = NZ // LANES
FIXED = 4 + 13 + 8
UNROLLS = (74, 72, 70, 68, 66, 64)


def split(row):
    return [row[:, LANES * j : LANES * (j + 1)] for j in range(TILES)]


def sideways(tiles, first, last):
    left = jnp.where(first, 0.0, pltpu.roll(tiles[3], 1, 1))
    right = jnp.where(last, 0.0, pltpu.roll(tiles[0], LANES - 1, 1))
    return [left + tiles[1], tiles[0] + tiles[2], tiles[1] + tiles[3], tiles[2] + right]


def kernel(*refs, shots):
    my_y = lax.rem(lax.axis_index("probe"), 4)
    source_row = NZ // 2 + EDGE - CHUNK * lax.axis_index("shot")
    n = len(refs) - FIXED
    slabs = refs[0 : n - 4]
    blocks = refs[n - 4 : n - 1]
    fields = refs[n - 1]
    outs = refs[n : n + 4]
    u_ref, edge_ref, sem, block_ref, block_sem, parity_ref, coef_ref, recv_ref, v_ref, e_ref, w_ref, grad_ref, back_ref, *d_refs = refs[n + 4 :]
    d_refs = [d_refs[4 * i : 4 * i + 4] for i in range(2)]

    lane = lax.broadcasted_iota(jnp.int32, (8, LANES), 1)
    first = lane == 0
    last = lane == LANES - 1

    half = shots // 2
    moves = [
        pltpu.make_async_copy(blocks[q], block_ref.at[q], block_sem.at[q]) for q in range(3)
    ]
    for n, target in enumerate((parity_ref, coef_ref, recv_ref, block_ref.at[3])):
        moves.append(pltpu.make_async_copy(fields.at[n], target, block_sem.at[3 + n]))
    for copy in moves:
        copy.start()
    copies = []
    if len(slabs) == 5:
        pieces = [(0, 0, shots), (1, 0, shots), (2, 0, half), (2, half, half), (3, 0, shots)]
    else:
        pieces = [(k, 0, shots) for k in range(4)]
    for slab, (k, first_shot, count) in zip(slabs, pieces):
        base = pl.multiple_of(EDGE + 16 * lax.rem(my_y + k, 4), 8)
        group = pl.ds(first_shot, count)
        for source, target in (
            (slab.at[:, :, 0:16, :], u_ref.at[group, 0:2, pl.ds(base, 16), :]),
            (slab.at[:, :, 16:24, :], edge_ref.at[k, group]),
        ):
            copies.append(pltpu.make_async_copy(source, target, sem.at[len(copies)]))
            copies[-1].start()

    back_ref[...] = match(NZ, None, back=True)
    for copy in moves:
        copy.wait()
    coef = coef_ref[...]
    e_ref[...] = 2.0 - 4.0 * coef
    w_ref[...] = recv_ref[...] * recv_ref[...]

    odd = parity_ref[...] > 0.5
    for q in range(4):
        w = block_ref[(q + 3) % 4]
        for colour in range(2):
            v = jnp.where(odd if colour else jnp.logical_not(odd), w, 0.0)
            for j, tile in enumerate(split(v)):
                v_ref.at[j][pl.ds(2 * q + colour, WIN, stride=8), :] = tile

    for copy in copies:
        copy.wait()
    for k in range(4):
        y = lax.rem(my_y + k, 4)

        @pl.when(y == 3)
        def _():
            u_ref[:, 0:2, 0:8, :] = edge_ref[k]

        @pl.when(y == 0)
        def _():
            u_ref[:, 0:2, 72:80, :] = edge_ref[k]
            u_ref[:, 5:7, 6:8, :] = edge_ref[k, :, :, 6:8, :]

    row = lax.broadcasted_iota(jnp.int32, (WIN, LANES), 0)
    column = lax.broadcasted_iota(jnp.int32, (WIN, LANES), 1)
    at_source = row == source_row
    for i in range(shots):
        for t in range(3):
            now = split(u_ref[i, t + 1])
            side = sideways(now, column == 0, column == LANES - 1)
            for j in range(TILES):
                here = slice(LANES * j, LANES * (j + 1))
                up = pltpu.roll(now[j], 1, 0)
                down = pltpu.roll(now[j], WIN - 1, 0)
                amp = u_ref[i, 5 + t // 2, 6 + t % 2 : 7 + t % 2, here]
                u_ref[i, t + 2, :, here] = (
                    e_ref[:, here] * now[j]
                    - u_ref[i, t, :, here]
                    + coef_ref[:, here] * (up + down + side[j])
                    + jnp.where(at_source, amp, 0.0)
                )

    def block(r):
        return pl.ds(pl.multiple_of(8 * r, 8), 8)

    def field(ref, r):
        return [ref[j, block(r), :] for j in range(TILES)]

    def wide(ref, r):
        return split(ref[pl.ds(r, 1), :])

    def store(ref, r, tiles):
        for j in range(TILES):
            ref[j, block(r), :] = tiles[j]

    def level(i, l, r):
        return split(u_ref[i, l + 1, pl.ds(r, 1), :])

    def times(a, b):
        return [p * q for p, q in zip(a, b)]

    def plus(a, b):
        return [p + q for p, q in zip(a, b)]

    def minus(a, b):
        return [p - q for p, q in zip(a, b)]

    def stencil(c, e, up, mid, down):
        side = sideways(mid, first, last)
        return plus(times(e, mid), times(c, plus(plus(up, down), side)))

    def sweeps(group):
        def source(i, r):
            return times(field(v_ref, r), level(2 * group + i, 0, r))

        def forward(t, r, carry):
            v = field(v_ref, r)
            c = wide(coef_ref, r)
            e = wide(e_ref, r)
            w = wide(w_ref, r) if t == 3 else None
            ahead = field(v_ref, r + 1) if t == 1 else None
            out = []
            for i in range(2):
                up, mid = carry[2 * i], carry[2 * i + 1]
                if t == 1:
                    down = times(ahead, level(2 * group + i, 0, r + 1))
                    store(d_refs[i][0], r + 1, down)
                else:
                    down = field(d_refs[i][t - 1], r + 1)
                new = plus(stencil(c, e, up, mid, down), times(v, level(2 * group + i, t, r)))
                if t >= 2:
                    new = minus(new, field(d_refs[i][t - 2], r))
                store(d_refs[i][t], r, times(w, new) if t == 3 else new)
                out += [mid, down]
            return out

        for t in range(1, 4):
            lo, hi = 2 + t, 78 - t
            init = []
            for i in range(2):
                if t == 1:
                    rows = [source(i, lo - 1), source(i, lo)]
                    store(d_refs[i][0], lo, rows[1])
                else:
                    rows = [field(d_refs[i][t - 1], lo - 1), field(d_refs[i][t - 1], lo)]
                init += rows
            lax.fori_loop(lo, hi, functools.partial(forward, t), init, unroll=UNROLLS[t - 1])

        def adjoint(t, r, carry):
            w = wide(w_ref, r)
            e = wide(e_ref, r)
            cn = wide(coef_ref, r + 1)
            out = []
            total = None
            for i in range(2):
                up, mid, here = carry[3 * i], carry[3 * i + 1], carry[3 * i + 2]
                below = field(d_refs[i][t + 1], r + 1)
                down = times(cn, below)
                side = sideways(mid, first, last)
                new = plus(times(w, field(d_refs[i][t], r)), times(e, here))
                new = plus(new, plus(plus(up, down), side))
                if t <= 1:
                    beyond = field(d_refs[i][t + 2], r)
                    new = minus(new, beyond)
                if t == 0:
                    final = field(d_refs[i][3], r)
                    for l, a in enumerate((new, here, beyond, final)):
                        term = times(a, level(2 * group + i, l, r))
                        total = term if total is None else plus(total, term)
                else:
                    store(d_refs[i][t], r, new)
                out += [mid, down, below]
            if t == 0:
                if group:
                    total = plus(total, field(grad_ref, r - EDGE))
                store(grad_ref, r - EDGE, total)
            return out

        for t in (2, 1, 0):
            lo, hi = 8 - t, 72 + t
            init = []
            c0, c1 = wide(coef_ref, lo - 1), wide(coef_ref, lo)
            for i in range(2):
                a0, a1 = field(d_refs[i][t + 1], lo - 1), field(d_refs[i][t + 1], lo)
                init += [times(c0, a0), times(c1, a1), a1]
            lax.fori_loop(lo, hi, functools.partial(adjoint, t), init, unroll=UNROLLS[5 - t])

    for group in range(shots // 2):
        sweeps(group)

    odd = parity_ref[EDGE : EDGE + CHUNK, :] > 0.5
    rows = []
    for q in range(4):
        tiles = []
        for j in range(TILES):
            even = grad_ref.at[j][pl.ds(2 * q, CHUNK, stride=8), :]
            other = grad_ref.at[j][pl.ds(2 * q + 1, CHUNK, stride=8), :]
            tiles.append(jnp.where(odd[:, LANES * j : LANES * (j + 1)], even, other))
        rows.append(jnp.concatenate(tiles, axis=1))
    result = exact_dot(jnp.concatenate(rows, axis=0), back_ref[...])
    for q in range(4):
        outs[q][...] = result[CHUNK * q : CHUNK * (q + 1)]


def apply(slabs, blocks, fields):
    shots = slabs[0].shape[0]
    vm = pl.BlockSpec(memory_space=pltpu.VMEM)
    anywhere = pl.BlockSpec(memory_space=pl.ANY)
    args = [*slabs, *blocks, fields]
    big = pltpu.VMEM((TILES, 8 * WIN, LANES), jnp.float32)
    return pl.pallas_call(
        functools.partial(kernel, shots=shots),
        out_shape=[jax.ShapeDtypeStruct((CHUNK, NZ), jnp.float32)] * 4,
        in_specs=[anywhere] * len(args),
        out_specs=[vm] * 4,
        scratch_shapes=[
            pltpu.VMEM((shots, 7, WIN, NZ), jnp.float32),
            pltpu.VMEM((4, shots, 2, 8, NZ), jnp.float32),
            pltpu.SemaphoreType.DMA((10,)),
            pltpu.VMEM((4, WIN, NZ), jnp.float32),
            pltpu.SemaphoreType.DMA((7,)),
            pltpu.VMEM((WIN, NZ), jnp.float32),
            pltpu.VMEM((WIN, NZ), jnp.float32),
            pltpu.VMEM((WIN, NZ), jnp.float32),
            big,
            pltpu.VMEM((WIN, NZ), jnp.float32),
            pltpu.VMEM((WIN, NZ), jnp.float32),
            pltpu.VMEM((TILES, 8 * CHUNK, LANES), jnp.float32),
            pltpu.VMEM((NZ, NZ), jnp.bfloat16),
        ]
        + [big] * 8,
        compiler_params=pltpu.CompilerParams(vmem_limit_bytes=32 * 1024 * 1024),
        cost_estimate=pl.CostEstimate(
            flops=shots * 8 * 8 * 70 * 512 * 12, bytes_accessed=4 << 20, transcendentals=0
        ),
        name="hessian_rows",
    )(*args)


def match(sources, column_of, back=False):
    shape = (sources, NZ)
    here = lax.broadcasted_iota(jnp.int32, shape, 0)
    there = lax.broadcasted_iota(jnp.int32, shape, 1)
    place, column = (here, there) if back else (there, column_of(here))
    kept = TILES * (place & (LANES - 1)) + (place >> 7)
    return jnp.where(column == kept, 1.0, 0.0).astype(jnp.bfloat16)


def exact_dot(a, b):
    high = a.astype(jnp.bfloat16)
    rest = a - high.astype(jnp.float32)
    middle = rest.astype(jnp.bfloat16)
    low = (rest - middle.astype(jnp.float32)).astype(jnp.bfloat16)
    x, y, z = (jnp.dot(part, b, preferred_element_type=jnp.float32) for part in (high, middle, low))
    return x + y + z


def emit_kernel(levels_ref, enc_ref, wav_ref, main_ref, edge_ref):
    y = lax.rem(lax.axis_index("probe"), 4)
    moved = exact_dot(levels_ref[...].reshape(64, NZ), match(NZ, lambda c: c))
    main_ref[...] = moved.reshape(2, 2, 16, NZ)
    signs = enc_ref[...].astype(jnp.float32)
    rows = [signs[i : i + 1] * wav_ref[t : t + 1, :] for i in range(2) for t in range(3)]
    rows += [jnp.zeros_like(rows[0])] * 2
    amps = exact_dot(jnp.concatenate(rows, axis=0), match(NSHOT, lambda k: 2 * k + 1))
    lowest = y == 0
    for i in range(2):
        for lev in range(2):
            base = 16 * (2 * i + lev)
            edge_ref[i, lev] = jnp.where(lowest, moved[base : base + 8], moved[base + 8 : base + 16])

    @pl.when(lowest)
    def _():
        for i in range(2):
            for t in range(3):
                row = 6 + t % 2
                edge_ref[i, t // 2, row : row + 1, :] = amps[3 * i + t : 3 * i + t + 1]


def emit(levels, encodings, wavelet):
    vm = pl.BlockSpec(memory_space=pltpu.VMEM)
    return pl.pallas_call(
        emit_kernel,
        out_shape=[
            jax.ShapeDtypeStruct((2, 2, 16, NZ), jnp.float32),
            jax.ShapeDtypeStruct((2, 2, 8, NZ), jnp.float32),
        ],
        in_specs=[vm] * 3,
        out_specs=[vm] * 2,
        name="own_rows",
    )(levels, encodings, wavelet)


def prepare_kernel(bounds_ref, probes, coefficient, receiver, *refs):
    mine_ref, fields_ref, pair, coef, recv, sem = refs
    chunk = lax.axis_index("shot")
    first = pl.multiple_of(chunk * CHUNK, 8)
    above = pl.multiple_of(jnp.maximum(first - EDGE, 0), 8)
    below = pl.multiple_of(jnp.minimum(first + CHUNK, NZ - EDGE), 8)
    copies = []
    for start, at, size in ((above, 0, EDGE), (first, EDGE, CHUNK), (below, EDGE + CHUNK, EDGE)):
        rows, spot = pl.ds(start, size), pl.ds(at, size)
        for source, target in (
            (probes.at[:, rows, :], pair.at[:, spot, :]),
            (coefficient.at[rows, :], coef.at[spot, :]),
            (receiver.at[rows, :], recv.at[spot, :]),
        ):
            copy = pltpu.make_async_copy(source, target, sem.at[len(copies)])
            copy.start()
            copies.append(copy)
    order = match(NZ, lambda c: c)
    row = chunk * CHUNK - EDGE + lax.broadcasted_iota(jnp.int32, (WIN, 65), 0)
    lane = lax.broadcasted_iota(jnp.int32, (WIN, 65), 1)
    counted = (row >= bounds_ref[...]) & (lane >= 1) & (lane <= 63)
    block = jnp.sum(jnp.where(counted, 1.0, 0.0), axis=1, keepdims=True)
    odd = block - 2.0 * jnp.floor(0.5 * block)
    odd = jnp.broadcast_to(odd, (WIN, NZ))
    fields_ref[0] = odd
    row = chunk * CHUNK - EDGE + lax.broadcasted_iota(jnp.int32, (WIN, NZ), 0)
    inside = (row >= 0) & (row < NZ)
    for copy in copies:
        copy.wait()
    mine = jnp.where(odd > 0.5, pair[1], pair[0])
    for n, value in enumerate((coef[...], recv[...], mine)):
        fields_ref[1 + n] = exact_dot(jnp.where(inside, value, 0.0), order)
    mine_ref[...] = fields_ref[3]


def prepare(bounds, probes, coefficient, receiver):
    vm = pl.BlockSpec(memory_space=pltpu.VMEM)
    hbm = pl.BlockSpec(memory_space=pl.ANY)
    field = pltpu.VMEM((WIN, NZ), jnp.float32)
    return pl.pallas_call(
        prepare_kernel,
        out_shape=[
            jax.ShapeDtypeStruct((WIN, NZ), jnp.float32),
            jax.ShapeDtypeStruct((4, WIN, NZ), jnp.float32),
        ],
        in_specs=[vm, hbm, hbm, hbm],
        out_specs=[vm] * 2,
        scratch_shapes=[
            pltpu.VMEM((2, WIN, NZ), jnp.float32),
            field,
            field,
            pltpu.SemaphoreType.DMA((9,)),
        ],
        cost_estimate=pl.CostEstimate(flops=0, bytes_accessed=12 << 20, transcendentals=0),
        name="own_windows",
    )(bounds, probes, coefficient, receiver)


AXES = ("shot", "probe")


def index(x, zh, y, zl, c):
    return (zl * 2 + c) * 32 + x * 8 + zh * 4 + y


def routes(source_of):
    pairs = []
    for x in range(4):
        for zh in range(2):
            for y in range(4):
                for zl in range(4):
                    for c in range(2):
                        source = source_of(x, zh, y, zl, c)
                        if source is not None:
                            pairs.append((index(*source), index(x, zh, y, zl, c)))
    return pairs


def main_source(k, x, zh, y, zl, c):
    return zl, c, y, x, zh ^ k


def edge_source(k, x, zh, y, zl, c):
    chunk = zl * 2 + c + {0: 1, 3: -1}.get(y, 8)
    if chunk < 0 or chunk > 7:
        return None
    return chunk // 2, chunk % 2, y, x, zh ^ k


def along_y(k):
    return routes(lambda x, zh, y, zl, c: (x, zh, (y + k) % 4, zl, c))


def along_x(k):
    return routes(lambda x, zh, y, zl, c: ((x + k) % 4, zh, y, zl, c))


def spread(array, along):
    far = lax.ppermute(array, AXES, along(2))
    return [array, lax.ppermute(array, AXES, along(1)), far, lax.ppermute(array, AXES, along(3))]


def on_device(
    probes, coarse_sample, coefficient, receiver, checkpoints, encodings, wavelet, bounds
):
    levels, edge = emit(checkpoints, encodings, wavelet)
    owns = []
    for k in range(2):
        main = lax.ppermute(levels, AXES, routes(functools.partial(main_source, k)))
        side = lax.ppermute(edge, AXES, routes(functools.partial(edge_source, k)))
        owns.append(jnp.concatenate([main, side], axis=2))

    mine, fields = prepare(
        bounds.reshape(1, 65), probes, coefficient, receiver
    )

    own, mine, fields = lax.optimization_barrier(
        (jnp.concatenate(owns, axis=0), mine, fields)
    )
    slabs = spread(own, along_y)
    blocks = spread(mine, along_x)

    terms = apply(slabs, blocks[1:], fields)
    parts = [terms[0]] + [lax.ppermute(terms[d], AXES, along_x(4 - d)) for d in (2, 1, 3)]
    total = parts[0] + parts[1] + parts[2] + parts[3]
    odd = fields[0, EDGE : EDGE + CHUNK] > 0.5
    keep = odd[None] != (jnp.arange(2) == 1)[:, None, None]
    return jnp.where(keep, total[None] - coarse_sample, 0.0)


def solution(mesh):
    return jax.shard_map(
        on_device,
        mesh=mesh,
        in_specs=(
            P("probe", None, None),
            P("probe", "shot", None),
            P(),
            P(),
            P("shot", None, "probe", None),
            P("shot", None),
            P(),
            P(),
        ),
        out_specs=P("probe", "shot", None),
        check_vma=False,
    )
```

```python
import functools
import jax
import jax.numpy as jnp
from jax import lax
from jax.experimental import pallas as pl
from jax.experimental.pallas import tpu as pltpu
from jax.sharding import PartitionSpec as P

NZ = 512
NSHOT = 256
CHUNK = 64
WIN = 80
EDGE = 8
LANES = 128
TILES = NZ // LANES
FIXED = 4 + 13 + 8
UNROLLS = (74, 72, 70, 68, 66, 64)


def split(row):
    return [row[:, LANES * j : LANES * (j + 1)] for j in range(TILES)]


def sideways(tiles, first, last):
    left = jnp.where(first, 0.0, pltpu.roll(tiles[3], 1, 1))
    right = jnp.where(last, 0.0, pltpu.roll(tiles[0], LANES - 1, 1))
    return [left + tiles[1], tiles[0] + tiles[2], tiles[1] + tiles[3], tiles[2] + right]


def kernel(*refs, shots):
    my_y = lax.rem(lax.axis_index("probe"), 4)
    source_row = NZ // 2 + EDGE - CHUNK * lax.axis_index("shot")
    n = len(refs) - FIXED
    slabs = refs[0 : n - 4]
    blocks = refs[n - 4 : n - 1]
    fields = refs[n - 1]
    outs = refs[n : n + 4]
    u_ref, edge_ref, sem, block_ref, block_sem, parity_ref, coef_ref, recv_ref, v_ref, e_ref, w_ref, grad_ref, back_ref, *d_refs = refs[n + 4 :]
    d_refs = [d_refs[4 * i : 4 * i + 4] for i in range(2)]

    lane = lax.broadcasted_iota(jnp.int32, (8, LANES), 1)
    first = lane == 0
    last = lane == LANES - 1

    half = shots // 2
    moves = [
        pltpu.make_async_copy(blocks[q], block_ref.at[q], block_sem.at[q]) for q in range(3)
    ]
    for n, target in enumerate((parity_ref, coef_ref, recv_ref, block_ref.at[3])):
        moves.append(pltpu.make_async_copy(fields.at[n], target, block_sem.at[3 + n]))
    for copy in moves:
        copy.start()
    copies = []
    if len(slabs) == 5:
        pieces = [(0, 0, shots), (1, 0, shots), (2, 0, half), (2, half, half), (3, 0, shots)]
    else:
        pieces = [(k, 0, shots) for k in range(4)]
    for slab, (k, first_shot, count) in zip(slabs, pieces):
        base = pl.multiple_of(EDGE + 16 * lax.rem(my_y + k, 4), 8)
        group = pl.ds(first_shot, count)
        for source, target in (
            (slab.at[:, :, 0:16, :], u_ref.at[group, 0:2, pl.ds(base, 16), :]),
            (slab.at[:, :, 16:24, :], edge_ref.at[k, group]),
        ):
            copies.append(pltpu.make_async_copy(source, target, sem.at[len(copies)]))
            copies[-1].start()

    back_ref[...] = match(NZ, None, back=True)
    for copy in moves:
        copy.wait()
    coef = coef_ref[...]
    e_ref[...] = 2.0 - 4.0 * coef
    w_ref[...] = recv_ref[...] * recv_ref[...]

    odd = parity_ref[...] > 0.5
    for q in range(4):
        w = block_ref[(q + 3) % 4]
        for colour in range(2):
            v = jnp.where(odd if colour else jnp.logical_not(odd), w, 0.0)
            for j, tile in enumerate(split(v)):
                v_ref.at[j][pl.ds(2 * q + colour, WIN, stride=8), :] = tile

    for copy in copies:
        copy.wait()
    for k in range(4):
        y = lax.rem(my_y + k, 4)

        @pl.when(y == 3)
        def _():
            u_ref[:, 0:2, 0:8, :] = edge_ref[k]

        @pl.when(y == 0)
        def _():
            u_ref[:, 0:2, 72:80, :] = edge_ref[k]
            u_ref[:, 5:7, 6:8, :] = edge_ref[k, :, :, 6:8, :]

    row = lax.broadcasted_iota(jnp.int32, (WIN, LANES), 0)
    column = lax.broadcasted_iota(jnp.int32, (WIN, LANES), 1)
    at_source = row == source_row
    for i in range(shots):
        for t in range(3):
            now = split(u_ref[i, t + 1])
            side = sideways(now, column == 0, column == LANES - 1)
            for j in range(TILES):
                here = slice(LANES * j, LANES * (j + 1))
                up = pltpu.roll(now[j], 1, 0)
                down = pltpu.roll(now[j], WIN - 1, 0)
                amp = u_ref[i, 5 + t // 2, 6 + t % 2 : 7 + t % 2, here]
                u_ref[i, t + 2, :, here] = (
                    e_ref[:, here] * now[j]
                    - u_ref[i, t, :, here]
                    + coef_ref[:, here] * (up + down + side[j])
                    + jnp.where(at_source, amp, 0.0)
                )

    def block(r):
        return pl.ds(pl.multiple_of(8 * r, 8), 8)

    def field(ref, r):
        return [ref[j, block(r), :] for j in range(TILES)]

    def wide(ref, r):
        return split(ref[pl.ds(r, 1), :])

    def store(ref, r, tiles):
        for j in range(TILES):
            ref[j, block(r), :] = tiles[j]

    def level(i, l, r):
        return split(u_ref[i, l + 1, pl.ds(r, 1), :])

    def times(a, b):
        return [p * q for p, q in zip(a, b)]

    def plus(a, b):
        return [p + q for p, q in zip(a, b)]

    def minus(a, b):
        return [p - q for p, q in zip(a, b)]

    def stencil(c, e, up, mid, down):
        side = sideways(mid, first, last)
        return plus(times(e, mid), times(c, plus(plus(up, down), side)))

    def sweeps(group):
        def source(i, r):
            return times(field(v_ref, r), level(2 * group + i, 0, r))

        def forward(t, r, carry):
            v = field(v_ref, r)
            c = wide(coef_ref, r)
            e = wide(e_ref, r)
            w = wide(w_ref, r) if t == 3 else None
            ahead = field(v_ref, r + 1) if t == 1 else None
            out = []
            for i in range(2):
                up, mid = carry[2 * i], carry[2 * i + 1]
                if t == 1:
                    down = times(ahead, level(2 * group + i, 0, r + 1))
                    store(d_refs[i][0], r + 1, down)
                else:
                    down = field(d_refs[i][t - 1], r + 1)
                new = plus(stencil(c, e, up, mid, down), times(v, level(2 * group + i, t, r)))
                if t >= 2:
                    new = minus(new, field(d_refs[i][t - 2], r))
                store(d_refs[i][t], r, times(w, new) if t == 3 else new)
                out += [mid, down]
            return out

        for t in range(1, 4):
            lo, hi = 2 + t, 78 - t
            init = []
            for i in range(2):
                if t == 1:
                    rows = [source(i, lo - 1), source(i, lo)]
                    store(d_refs[i][0], lo, rows[1])
                else:
                    rows = [field(d_refs[i][t - 1], lo - 1), field(d_refs[i][t - 1], lo)]
                init += rows
            lax.fori_loop(lo, hi, functools.partial(forward, t), init, unroll=UNROLLS[t - 1])

        def adjoint(t, r, carry):
            w = wide(w_ref, r)
            e = wide(e_ref, r)
            cn = wide(coef_ref, r + 1)
            out = []
            total = None
            for i in range(2):
                up, mid, here = carry[3 * i], carry[3 * i + 1], carry[3 * i + 2]
                below = field(d_refs[i][t + 1], r + 1)
                down = times(cn, below)
                side = sideways(mid, first, last)
                new = plus(times(w, field(d_refs[i][t], r)), times(e, here))
                new = plus(new, plus(plus(up, down), side))
                if t <= 1:
                    beyond = field(d_refs[i][t + 2], r)
                    new = minus(new, beyond)
                if t == 0:
                    final = field(d_refs[i][3], r)
                    for l, a in enumerate((new, here, beyond, final)):
                        term = times(a, level(2 * group + i, l, r))
                        total = term if total is None else plus(total, term)
                else:
                    store(d_refs[i][t], r, new)
                out += [mid, down, below]
            if t == 0:
                if group:
                    total = plus(total, field(grad_ref, r - EDGE))
                store(grad_ref, r - EDGE, total)
            return out

        for t in (2, 1, 0):
            lo, hi = 8 - t, 72 + t
            init = []
            c0, c1 = wide(coef_ref, lo - 1), wide(coef_ref, lo)
            for i in range(2):
                a0, a1 = field(d_refs[i][t + 1], lo - 1), field(d_refs[i][t + 1], lo)
                init += [times(c0, a0), times(c1, a1), a1]
            lax.fori_loop(lo, hi, functools.partial(adjoint, t), init, unroll=UNROLLS[5 - t])

    for group in range(shots // 2):
        sweeps(group)

    odd = parity_ref[EDGE : EDGE + CHUNK, :] > 0.5
    rows = []
    for q in range(4):
        tiles = []
        for j in range(TILES):
            even = grad_ref.at[j][pl.ds(2 * q, CHUNK, stride=8), :]
            other = grad_ref.at[j][pl.ds(2 * q + 1, CHUNK, stride=8), :]
            tiles.append(jnp.where(odd[:, LANES * j : LANES * (j + 1)], even, other))
        rows.append(jnp.concatenate(tiles, axis=1))
    result = exact_dot(jnp.concatenate(rows, axis=0), back_ref[...])
    for q in range(4):
        outs[q][...] = result[CHUNK * q : CHUNK * (q + 1)]


def apply(slabs, blocks, fields):
    shots = slabs[0].shape[0]
    vm = pl.BlockSpec(memory_space=pltpu.VMEM)
    anywhere = pl.BlockSpec(memory_space=pl.ANY)
    args = [*slabs, *blocks, fields]
    big = pltpu.VMEM((TILES, 8 * WIN, LANES), jnp.float32)
    return pl.pallas_call(
        functools.partial(kernel, shots=shots),
        out_shape=[jax.ShapeDtypeStruct((CHUNK, NZ), jnp.float32)] * 4,
        in_specs=[anywhere] * len(args),
        out_specs=[vm] * 4,
        scratch_shapes=[
            pltpu.VMEM((shots, 7, WIN, NZ), jnp.float32),
            pltpu.VMEM((4, shots, 2, 8, NZ), jnp.float32),
            pltpu.SemaphoreType.DMA((10,)),
            pltpu.VMEM((4, WIN, NZ), jnp.float32),
            pltpu.SemaphoreType.DMA((7,)),
            pltpu.VMEM((WIN, NZ), jnp.float32),
            pltpu.VMEM((WIN, NZ), jnp.float32),
            pltpu.VMEM((WIN, NZ), jnp.float32),
            big,
            pltpu.VMEM((WIN, NZ), jnp.float32),
            pltpu.VMEM((WIN, NZ), jnp.float32),
            pltpu.VMEM((TILES, 8 * CHUNK, LANES), jnp.float32),
            pltpu.VMEM((NZ, NZ), jnp.bfloat16),
        ]
        + [big] * 8,
        compiler_params=pltpu.CompilerParams(vmem_limit_bytes=32 * 1024 * 1024),
        cost_estimate=pl.CostEstimate(
            flops=shots * 8 * 8 * 70 * 512 * 12, bytes_accessed=4 << 20, transcendentals=0
        ),
        name="hessian_rows",
    )(*args)


def match(sources, column_of, back=False):
    shape = (sources, NZ)
    here = lax.broadcasted_iota(jnp.int32, shape, 0)
    there = lax.broadcasted_iota(jnp.int32, shape, 1)
    place, column = (here, there) if back else (there, column_of(here))
    kept = TILES * (place & (LANES - 1)) + (place >> 7)
    return jnp.where(column == kept, 1.0, 0.0).astype(jnp.bfloat16)


def exact_dot(a, b):
    high = a.astype(jnp.bfloat16)
    rest = a - high.astype(jnp.float32)
    middle = rest.astype(jnp.bfloat16)
    low = (rest - middle.astype(jnp.float32)).astype(jnp.bfloat16)
    x, y, z = (jnp.dot(part, b, preferred_element_type=jnp.float32) for part in (high, middle, low))
    return x + y + z


def emit_kernel(levels_ref, enc_ref, wav_ref, main_ref, edge_ref):
    y = lax.rem(lax.axis_index("probe"), 4)
    moved = exact_dot(levels_ref[...].reshape(64, NZ), match(NZ, lambda c: c))
    main_ref[...] = moved.reshape(2, 2, 16, NZ)
    signs = enc_ref[...].astype(jnp.float32)
    rows = [signs[i : i + 1] * wav_ref[t : t + 1, :] for i in range(2) for t in range(3)]
    rows += [jnp.zeros_like(rows[0])] * 2
    amps = exact_dot(jnp.concatenate(rows, axis=0), match(NSHOT, lambda k: 2 * k + 1))
    lowest = y == 0
    for i in range(2):
        for lev in range(2):
            base = 16 * (2 * i + lev)
            edge_ref[i, lev] = jnp.where(lowest, moved[base : base + 8], moved[base + 8 : base + 16])

    @pl.when(lowest)
    def _():
        for i in range(2):
            for t in range(3):
                row = 6 + t % 2
                edge_ref[i, t // 2, row : row + 1, :] = amps[3 * i + t : 3 * i + t + 1]


def emit(levels, encodings, wavelet):
    vm = pl.BlockSpec(memory_space=pltpu.VMEM)
    return pl.pallas_call(
        emit_kernel,
        out_shape=[
            jax.ShapeDtypeStruct((2, 2, 16, NZ), jnp.float32),
            jax.ShapeDtypeStruct((2, 2, 8, NZ), jnp.float32),
        ],
        in_specs=[vm] * 3,
        out_specs=[vm] * 2,
        name="own_rows",
    )(levels, encodings, wavelet)


def prepare_kernel(bounds_ref, probes, coefficient, receiver, *refs):
    mine_ref, fields_ref, pair, coef, recv, sem = refs
    chunk = lax.axis_index("shot")
    first = pl.multiple_of(chunk * CHUNK, 8)
    above = pl.multiple_of(jnp.maximum(first - EDGE, 0), 8)
    below = pl.multiple_of(jnp.minimum(first + CHUNK, NZ - EDGE), 8)
    copies = []
    for start, at, size in ((above, 0, EDGE), (first, EDGE, CHUNK), (below, EDGE + CHUNK, EDGE)):
        rows, spot = pl.ds(start, size), pl.ds(at, size)
        for source, target in (
            (probes.at[:, rows, :], pair.at[:, spot, :]),
            (coefficient.at[rows, :], coef.at[spot, :]),
            (receiver.at[rows, :], recv.at[spot, :]),
        ):
            copy = pltpu.make_async_copy(source, target, sem.at[len(copies)])
            copy.start()
            copies.append(copy)
    order = match(NZ, lambda c: c)
    row = chunk * CHUNK - EDGE + lax.broadcasted_iota(jnp.int32, (WIN, 65), 0)
    lane = lax.broadcasted_iota(jnp.int32, (WIN, 65), 1)
    counted = (row >= bounds_ref[...]) & (lane >= 1) & (lane <= 63)
    block = jnp.sum(jnp.where(counted, 1.0, 0.0), axis=1, keepdims=True)
    odd = block - 2.0 * jnp.floor(0.5 * block)
    odd = jnp.broadcast_to(odd, (WIN, NZ))
    fields_ref[0] = odd
    row = chunk * CHUNK - EDGE + lax.broadcasted_iota(jnp.int32, (WIN, NZ), 0)
    inside = (row >= 0) & (row < NZ)
    for copy in copies:
        copy.wait()
    mine = jnp.where(odd > 0.5, pair[1], pair[0])
    for n, value in enumerate((coef[...], recv[...], mine)):
        fields_ref[1 + n] = exact_dot(jnp.where(inside, value, 0.0), order)
    mine_ref[...] = fields_ref[3]


def prepare(bounds, probes, coefficient, receiver):
    vm = pl.BlockSpec(memory_space=pltpu.VMEM)
    hbm = pl.BlockSpec(memory_space=pl.ANY)
    field = pltpu.VMEM((WIN, NZ), jnp.float32)
    return pl.pallas_call(
        prepare_kernel,
        out_shape=[
            jax.ShapeDtypeStruct((WIN, NZ), jnp.float32),
            jax.ShapeDtypeStruct((4, WIN, NZ), jnp.float32),
        ],
        in_specs=[vm, hbm, hbm, hbm],
        out_specs=[vm] * 2,
        scratch_shapes=[
            pltpu.VMEM((2, WIN, NZ), jnp.float32),
            field,
            field,
            pltpu.SemaphoreType.DMA((9,)),
        ],
        cost_estimate=pl.CostEstimate(flops=0, bytes_accessed=12 << 20, transcendentals=0),
        name="own_windows",
    )(bounds, probes, coefficient, receiver)


AXES = ("shot", "probe")


def index(x, zh, y, zl, c):
    return (zl * 2 + c) * 32 + x * 8 + zh * 4 + y


def routes(source_of):
    pairs = []
    for x in range(4):
        for zh in range(2):
            for y in range(4):
                for zl in range(4):
                    for c in range(2):
                        source = source_of(x, zh, y, zl, c)
                        if source is not None:
                            pairs.append((index(*source), index(x, zh, y, zl, c)))
    return pairs


def main_source(k, x, zh, y, zl, c):
    return zl, c, y, x, zh ^ k


def edge_source(k, x, zh, y, zl, c):
    chunk = zl * 2 + c + {0: 1, 3: -1}.get(y, 8)
    if chunk < 0 or chunk > 7:
        return None
    return chunk // 2, chunk % 2, y, x, zh ^ k


def along_y(k):
    return routes(lambda x, zh, y, zl, c: (x, zh, (y + k) % 4, zl, c))


def along_x(k):
    return routes(lambda x, zh, y, zl, c: ((x + k) % 4, zh, y, zl, c))


def spread(array, along):
    far = lax.ppermute(array, AXES, along(2))
    return [array, lax.ppermute(array, AXES, along(1)), far, lax.ppermute(array, AXES, along(3))]


def on_device(
    probes, coarse_sample, coefficient, receiver, checkpoints, encodings, wavelet, bounds
):
    levels, edge = emit(checkpoints, encodings, wavelet)
    owns = []
    for k in range(2):
        main = lax.ppermute(levels, AXES, routes(functools.partial(main_source, k)))
        side = lax.ppermute(edge, AXES, routes(functools.partial(edge_source, k)))
        owns.append(jnp.concatenate([main, side], axis=2))

    mine, fields = prepare(
        bounds.reshape(1, 65), probes, coefficient, receiver
    )

    own, mine, fields = lax.optimization_barrier(
        (jnp.concatenate(owns, axis=0), mine, fields)
    )
    slabs = spread(own, along_y)
    blocks = spread(mine, along_x)

    terms = apply(slabs, blocks[1:], fields)
    parts = [terms[0]] + [lax.ppermute(terms[d], AXES, along_x(4 - d)) for d in (1, 2, 3)]
    total = parts[0] + parts[1] + parts[2] + parts[3]
    odd = fields[0, EDGE : EDGE + CHUNK] > 0.5
    keep = odd[None] != (jnp.arange(2) == 1)[:, None, None]
    return jnp.where(keep, total[None] - coarse_sample, 0.0)


def solution(mesh):
    return jax.shard_map(
        on_device,
        mesh=mesh,
        in_specs=(
            P("probe", None, None),
            P("probe", "shot", None),
            P(),
            P(),
            P("shot", None, "probe", None),
            P("shot", None),
            P(),
            P(),
        ),
        out_specs=P("probe", "shot", None),
        check_vma=False,
    )
```
